256 devices in a mesh: gx: 8 (over z_lo, y), gy: 4 (over z_hi), gz: 8 (over x, core).
Axes of the slice: x: 4, y: 4, z: 8 (z_hi: 4, z_lo: 2; z = z_hi * 2 + z_lo), core: 2. Of those that a mesh axis runs over, the one named last changes fastest.
Arguments:
- tokens: bfloat16 [1024, 12288], P(('gy', 'gz'), 'gx'), may hold values from -6 to 6
- weight_in: bfloat16 [12288, 24576], P('gx', ('gy', 'gz')), may hold values from -0.0546875 to 0.0546875
- bias_hidden: float32 [24576], P(('gy', 'gz')), may hold values from -3 to 3
- weight_out: bfloat16 [24576, 12288], P(('gy', 'gz'), 'gx'), may hold values from -0.0390625 to 0.0390625
- grad_output: bfloat16 [1024, 12288], P(('gy', 'gz'), 'gx'), may hold values from -6 to 6
Outputs:
- grad_tokens: bfloat16 [1024, 12288], P(('gy', 'gz'), 'gx')
- grad_weight_in: bfloat16 [12288, 24576], P('gx', ('gy', 'gz'))
- grad_weight_out: bfloat16 [24576, 12288], P(('gy', 'gz'), 'gx')
The draws below stay inside these ranges and needn't reach their ends.
All inputs are finite; a program needn't handle non-finite values.
Results may differ from the reference program's by a relative error of at most 0.005.
Values may be sent and summed in bfloat16 or wider, within the bound.
No kernel may reach another device: no remote copies, remote signals or barrier semaphores. Data moves between devices by JAX's collectives and lax.ppermute only.
A program may use at most 128 MiB of HBM per device.

```python
import math
import jax
import jax.numpy as jnp

D = 12288
FF = 24576
TOKENS = 1024


def steps_of(stream_key, extent, pieces, smallest, largest):
    factor_of, own = 1.0, jax.random.fold_in(stream_key, 6)
    for dim, blocks in pieces:
        steps = jnp.exp(jax.random.uniform(jax.random.fold_in(own, dim), (blocks,), jnp.float32, smallest / len(pieces), largest / len(pieces)))
        factor_of = factor_of * jnp.repeat(steps, extent[dim] // blocks).reshape([-1 if axis == dim else 1 for axis in range(len(extent))])
    return factor_of


def gaussian(key, dims, spread, limit, split=(), held_as=jnp.bfloat16):
    array = spread * jax.random.normal(key, dims, jnp.float32)
    if split:
        array = array * steps_of(key, dims, split, -0.22, 0.18)
    return jnp.clip(array, -limit, limit).astype(held_as)


def setup_inputs(seed: int = 0) -> dict:
    splits = jax.random.split(jax.random.key(seed), 6)
    tokens = gaussian(splits[0], (TOKENS, D), 1.0, 6.0, ((0, 32), (1, 8)))
    weight_in = gaussian(splits[1], (D, FF), D ** -0.5, 0.0546875, ((0, 8), (1, 32)))
    bias_hidden = gaussian(splits[2], (FF,), 0.5, 3.0, ((0, 32),), jnp.float32)
    weight_out = gaussian(splits[3], (FF, D), FF ** -0.5, 0.0390625, ((0, 32), (1, 8)))
    grad_output = gaussian(splits[4], (TOKENS, D), 1.0, 6.0, ((0, 32), (1, 8)))
    return dict(tokens=tokens, weight_in=weight_in, bias_hidden=bias_hidden, weight_out=weight_out, grad_output=grad_output)


root_coef = math.sqrt(2.0 / math.pi)
cubic_coef = 0.044715

def gelu_pair(pre_act, upstream):
    tanh_part = jnp.tanh(root_coef * (pre_act + cubic_coef * pre_act * pre_act * pre_act))
    activation = 0.5 * pre_act * (1.0 + tanh_part)
    slope_value = 0.5 * (1.0 + tanh_part) + 0.5 * pre_act * (1.0 - tanh_part * tanh_part) * root_coef * (1.0 + 3.0 * cubic_coef * pre_act * pre_act)
    return (activation.astype(jnp.bfloat16), (upstream * slope_value).astype(jnp.bfloat16))

def reference(tokens, weight_in, bias_hidden, weight_out, grad_output):
    pre_act = jnp.dot(tokens, weight_in, preferred_element_type=jnp.float32) + bias_hidden
    upstream = jnp.dot(grad_output, weight_out.T, preferred_element_type=jnp.float32)
    activation, grad_hidden = gelu_pair(pre_act, upstream)
    grad_tokens = jnp.dot(grad_hidden, weight_in.T, preferred_element_type=jnp.float32).astype(jnp.bfloat16)
    norm_scale = 1.0 / math.sqrt(TOKENS)
    grad_weight_in = (jnp.dot(tokens.T, grad_hidden, preferred_element_type=jnp.float32) * norm_scale).astype(jnp.bfloat16)
    grad_weight_out = (jnp.dot(activation.T, grad_output, preferred_element_type=jnp.float32) * norm_scale).astype(jnp.bfloat16)
    return (grad_tokens, grad_weight_in, grad_weight_out)
```

```python
import math

import jax
import jax.numpy as jnp
from jax import lax
from jax.sharding import PartitionSpec as P

root_coef = math.sqrt(2.0 / math.pi)
cubic_coef = 0.044715
bf16 = jnp.bfloat16
f32 = jnp.float32


def gelu_pair(pre_act, upstream):
    tanh_part = jnp.tanh(root_coef * (pre_act + cubic_coef * pre_act * pre_act * pre_act))
    activation = 0.5 * pre_act * (1.0 + tanh_part)
    slope_value = 0.5 * (1.0 + tanh_part) + 0.5 * pre_act * (
        1.0 - tanh_part * tanh_part
    ) * root_coef * (1.0 + 3.0 * cubic_coef * pre_act * pre_act)
    return (activation.astype(bf16), (upstream * slope_value).astype(bf16))


def contract_last(left, right):
    return lax.dot_general(left, right, (((1,), (1,)), ((), ())), preferred_element_type=f32)


def contract_first(left, right):
    return lax.dot_general(left, right, (((0,), (0,)), ((), ())), preferred_element_type=f32)


def solution(mesh):
    n_x, n_y, n_z = (mesh.shape[a] for a in ("gx", "gy", "gz"))

    def shift_y(a, k):
        return lax.ppermute(a, "gy", [(i, (i + k) % n_y) for i in range(n_y)])

    def shift_chip(a, k):
        return lax.ppermute(a, "gz", [(i, (i + 2 * k) % n_z) for i in range(n_z)])

    def swap_core(a):
        return lax.ppermute(a, "gz", [(i, i ^ 1) for i in range(n_z)])

    def gather_rows(a):
        a = jnp.concatenate([a] + [shift_y(a, k) for k in range(1, n_y)], axis=0)
        a = jnp.concatenate([a] + [shift_chip(a, k) for k in range(1, n_z // 2)], axis=0)
        return jnp.concatenate([a, swap_core(a)], axis=0)

    def scatter_rows(a):
        half = a.shape[0] // 2
        a = a[:half] + swap_core(a[half:].astype(bf16)).astype(f32)
        for shift, n in ((shift_chip, n_z // 2), (shift_y, n_y)):
            rows = a.shape[0] // n
            total = a[:rows]
            for k in range(1, n):
                part = a[k * rows : (k + 1) * rows].astype(bf16)
                total = total + shift(part, -k).astype(f32)
            a = total
        return a.astype(bf16)

    def sum_width(part):
        part = part.astype(bf16).reshape(n_x, part.shape[0] // n_x, part.shape[1])
        parts = lax.all_to_all(part, "gx", 0, 0, tiled=True)
        return jnp.sum(parts.astype(f32), axis=0)

    def gather_width(share):
        copies = jnp.broadcast_to(share[None], (n_x, *share.shape))
        parts = lax.all_to_all(copies, "gx", 0, 0, tiled=True)
        return parts.reshape(-1, share.shape[1])

    def shards(tokens, weight_in, bias_hidden, weight_out, grad_output):
        tokens_all = gather_rows(tokens)
        grad_all = gather_rows(grad_output)
        norm_scale = 1.0 / math.sqrt(tokens_all.shape[0])
        pre_act = sum_width(jnp.dot(tokens_all, weight_in, preferred_element_type=f32)) + bias_hidden
        upstream = sum_width(contract_last(grad_all, weight_out))
        act_share, grad_share = gelu_pair(pre_act, upstream)
        grad_hidden = gather_width(grad_share)
        grad_tokens = scatter_rows(contract_last(grad_hidden, weight_in))
        activation = gather_width(act_share)
        grad_weight_in = (contract_first(tokens_all, grad_hidden) * norm_scale).astype(bf16)
        grad_weight_out = (contract_first(activation, grad_all) * norm_scale).astype(bf16)
        return (grad_tokens, grad_weight_in, grad_weight_out)

    return jax.shard_map(
        shards,
        mesh=mesh,
        in_specs=(
            P(("gy", "gz"), "gx"),
            P("gx", ("gy", "gz")),
            P(("gy", "gz")),
            P(("gy", "gz"), "gx"),
            P(("gy", "gz"), "gx"),
        ),
        out_specs=(P(("gy", "gz"), "gx"), P("gx", ("gy", "gz")), P(("gy", "gz"), "gx")),
        check_vma=False,
    )
```

```python
import math

import jax
import jax.numpy as jnp
from jax import lax
from jax.sharding import PartitionSpec as P

root_coef = math.sqrt(2.0 / math.pi)
cubic_coef = 0.044715
bf16 = jnp.bfloat16
f32 = jnp.float32


def gelu_pair(pre_act, upstream):
    tanh_part = jnp.tanh(root_coef * (pre_act + cubic_coef * pre_act * pre_act * pre_act))
    activation = 0.5 * pre_act * (1.0 + tanh_part)
    slope_value = 0.5 * (1.0 + tanh_part) + 0.5 * pre_act * (
        1.0 - tanh_part * tanh_part
    ) * root_coef * (1.0 + 3.0 * cubic_coef * pre_act * pre_act)
    return (activation.astype(bf16), (upstream * slope_value).astype(bf16))


def contract_last(left, right):
    return lax.dot_general(left, right, (((1,), (1,)), ((), ())), preferred_element_type=f32)


def contract_first(left, right):
    return lax.dot_general(left, right, (((0,), (0,)), ((), ())), preferred_element_type=f32)


def solution(mesh):
    n_x, n_y, n_z = (mesh.shape[a] for a in ("gx", "gy", "gz"))

    def shift_y(a, k):
        return lax.ppermute(a, "gy", [(i, (i + k) % n_y) for i in range(n_y)])

    def shift_chip(a, k):
        return lax.ppermute(a, "gz", [(i, (i + 2 * k) % n_z) for i in range(n_z)])

    def swap_core(a):
        return lax.ppermute(a, "gz", [(i, i ^ 1) for i in range(n_z)])

    def gather_far(a):
        return jnp.concatenate([a] + [shift_y(a, k) for k in range(1, n_y)], axis=0)

    def chips(a):
        return [shift_chip(a, k) for k in range(1, n_z // 2)]

    def scatter_rows(a):
        for shift, n in ((shift_chip, n_z // 2), (shift_y, n_y)):
            rows = a.shape[0] // n
            total = a[:rows]
            for k in range(1, n):
                part = a[k * rows : (k + 1) * rows].astype(bf16)
                total = total + shift(part, -k).astype(f32)
            a = total
        return a.astype(bf16)

    def sum_width(part):
        part = part.astype(bf16).reshape(n_x, part.shape[0] // n_x, part.shape[1])
        parts = lax.all_to_all(part, "gx", 0, 0, tiled=True)
        return jnp.sum(parts.astype(f32), axis=0)

    def gather_width(share):
        copies = jnp.broadcast_to(share[None], (n_x, *share.shape))
        parts = lax.all_to_all(copies, "gx", 0, 0, tiled=True)
        return parts.reshape(-1, share.shape[1])

    def after(a, *others):
        return lax.optimization_barrier((a, *others))[0]

    def shards(tokens, weight_in, bias_hidden, weight_out, grad_output):
        tokens_far = gather_far(tokens)
        grad_far = gather_far(after(grad_output, tokens_far))
        tokens_near = jnp.concatenate([tokens_far] + chips(tokens_far), axis=0)
        grad_chips = chips(after(grad_far, tokens_near))
        tokens_all = jnp.concatenate([tokens_near, swap_core(tokens_near)], axis=0)
        total_rows = tokens_all.shape[0]
        half = total_rows // 2
        norm_scale = 1.0 / math.sqrt(total_rows)
        pre_part = jnp.dot(tokens_all, weight_in, preferred_element_type=f32).astype(bf16)
        pre_act = sum_width(pre_part) + bias_hidden
        grad_chips = [after(a, pre_part) for a in grad_chips]
        grad_near = jnp.concatenate([grad_far] + grad_chips, axis=0)
        grad_all = jnp.concatenate([grad_near, swap_core(grad_near)], axis=0)
        upstream = sum_width(contract_last(grad_all, weight_out))
        act_share, grad_share = gelu_pair(pre_act, upstream)
        grad_hidden = gather_width(grad_share)
        other = contract_last(grad_hidden[half:], weight_in).astype(bf16)
        own = contract_last(grad_hidden[:half], weight_in)
        activation = gather_width(after(act_share, other, own))
        grad_tokens = scatter_rows(own + swap_core(other).astype(f32))
        grad_weight_in = (contract_first(tokens_all, grad_hidden) * norm_scale).astype(bf16)
        grad_weight_out = (contract_first(activation, grad_all) * norm_scale).astype(bf16)
        return (grad_tokens, grad_weight_in, grad_weight_out)

    return jax.shard_map(
        shards,
        mesh=mesh,
        in_specs=(
            P(("gy", "gz"), "gx"),
            P("gx", ("gy", "gz")),
            P(("gy", "gz")),
            P(("gy", "gz"), "gx"),
            P(("gy", "gz"), "gx"),
        ),
        out_specs=(P(("gy", "gz"), "gx"), P("gx", ("gy", "gz")), P(("gy", "gz"), "gx")),
        check_vma=False,
    )
```

```python
import math

import jax
import jax.numpy as jnp
from jax import lax
from jax.sharding import PartitionSpec as P

root_coef = math.sqrt(2.0 / math.pi)
cubic_coef = 0.044715
bf16 = jnp.bfloat16
f32 = jnp.float32


def gelu_pair(pre_act, upstream):
    tanh_part = jnp.tanh(root_coef * (pre_act + cubic_coef * pre_act * pre_act * pre_act))
    activation = 0.5 * pre_act * (1.0 + tanh_part)
    slope_value = 0.5 * (1.0 + tanh_part) + 0.5 * pre_act * (
        1.0 - tanh_part * tanh_part
    ) * root_coef * (1.0 + 3.0 * cubic_coef * pre_act * pre_act)
    return (activation.astype(bf16), (upstream * slope_value).astype(bf16))


def contract_last(left, right):
    return lax.dot_general(left, right, (((1,), (1,)), ((), ())), preferred_element_type=f32)


def contract_first(left, right):
    return lax.dot_general(left, right, (((0,), (0,)), ((), ())), preferred_element_type=f32)


def solution(mesh):
    n_x, n_y, n_z = (mesh.shape[a] for a in ("gx", "gy", "gz"))

    def shift_y(a, k):
        return lax.ppermute(a, "gy", [(i, (i + k) % n_y) for i in range(n_y)])

    def shift_chip(a, k):
        return lax.ppermute(a, "gz", [(i, (i + 2 * k) % n_z) for i in range(n_z)])

    def swap_core(a):
        return lax.ppermute(a, "gz", [(i, i ^ 1) for i in range(n_z)])

    def groups(a):
        return [shift_y(a, k) for k in range(1, n_y)]

    def chips(a):
        return [shift_chip(a, k) for k in range(1, n_z // 2)]

    def scatter_stage(a, shift, n, beside):
        rows = a.shape[0] // n
        sent = [shift(a[k * rows : (k + 1) * rows].astype(bf16), -k) for k in range(1, n)]
        sent, beside = lax.optimization_barrier((sent, beside))
        total = a[:rows]
        for part in sent:
            total = total + part.astype(f32)
        return total, beside

    def sum_width(part):
        part = part.astype(bf16).reshape(n_x, part.shape[0] // n_x, part.shape[1])
        parts = lax.all_to_all(part, "gx", 0, 0, tiled=True)
        return jnp.sum(parts.astype(f32), axis=0)

    def gather_width(share):
        copies = jnp.broadcast_to(share[None], (n_x, *share.shape))
        parts = lax.all_to_all(copies, "gx", 0, 0, tiled=True)
        return parts.reshape(-1, share.shape[1])

    def after(a, *others):
        return lax.optimization_barrier((a, *others))[0]

    def shards(tokens, weight_in, bias_hidden, weight_out, grad_output):
        tokens_far = jnp.concatenate([tokens] + groups(tokens), axis=0)
        grad_groups = groups(after(grad_output, tokens_far))
        tokens_chips, grad_groups = lax.optimization_barrier((chips(tokens_far), grad_groups))
        grad_far = jnp.concatenate([grad_output] + grad_groups, axis=0)
        tokens_near = jnp.concatenate([tokens_far] + tokens_chips, axis=0)
        tokens_all = jnp.concatenate([tokens_near, swap_core(tokens_near)], axis=0)
        total_rows = tokens_all.shape[0]
        half = total_rows // 2
        norm_scale = 1.0 / math.sqrt(total_rows)
        pre_part = jnp.dot(tokens_all, weight_in, preferred_element_type=f32).astype(bf16)
        pre_act = sum_width(pre_part) + bias_hidden
        last = n_z // 4
        grad_chips = [
            shift_chip(after(grad_far, pre_part) if k == last else grad_far, k)
            for k in range(1, n_z // 2)
        ]
        grad_near = jnp.concatenate([grad_far] + grad_chips, axis=0)
        grad_all = jnp.concatenate([grad_near, swap_core(grad_near)], axis=0)
        upstream = sum_width(contract_last(grad_all, weight_out))
        act_share, grad_share = gelu_pair(pre_act, upstream)
        grad_hidden = gather_width(grad_share)
        other = contract_last(grad_hidden[half:], weight_in).astype(bf16)
        own = contract_last(grad_hidden[:half], weight_in)
        activation = gather_width(after(act_share, other, own))
        grad_weight_in = (contract_first(tokens_all, grad_hidden) * norm_scale).astype(bf16)
        grad_weight_out = (contract_first(activation, grad_all) * norm_scale).astype(bf16)
        own = own + swap_core(other).astype(f32)
        own, grad_weight_in = scatter_stage(own, shift_chip, n_z // 2, grad_weight_in)
        own, grad_weight_out = scatter_stage(own, shift_y, n_y, grad_weight_out)
        return (own.astype(bf16), grad_weight_in, grad_weight_out)

    return jax.shard_map(
        shards,
        mesh=mesh,
        in_specs=(
            P(("gy", "gz"), "gx"),
            P("gx", ("gy", "gz")),
            P(("gy", "gz")),
            P(("gy", "gz"), "gx"),
            P(("gy", "gz"), "gx"),
        ),
        out_specs=(P(("gy", "gz"), "gx"), P("gx", ("gy", "gz")), P(("gy", "gz"), "gx")),
        check_vma=False,
    )
```

```python
import math

import jax
import jax.numpy as jnp
from jax import lax
from jax.sharding import PartitionSpec as P

root_coef = math.sqrt(2.0 / math.pi)
cubic_coef = 0.044715
bf16 = jnp.bfloat16
f32 = jnp.float32


def gelu_pair(pre_act, upstream):
    tanh_part = jnp.tanh(root_coef * (pre_act + cubic_coef * pre_act * pre_act * pre_act))
    activation = 0.5 * pre_act * (1.0 + tanh_part)
    slope_value = 0.5 * (1.0 + tanh_part) + 0.5 * pre_act * (
        1.0 - tanh_part * tanh_part
    ) * root_coef * (1.0 + 3.0 * cubic_coef * pre_act * pre_act)
    return (activation.astype(bf16), (upstream * slope_value).astype(bf16))


def contract_last(left, right):
    return lax.dot_general(left, right, (((1,), (1,)), ((), ())), preferred_element_type=f32)


def contract_first(left, right):
    return lax.dot_general(left, right, (((0,), (0,)), ((), ())), preferred_element_type=f32)


def solution(mesh):
    n_x, n_y, n_z = (mesh.shape[a] for a in ("gx", "gy", "gz"))

    def shift_y(a, k):
        return lax.ppermute(a, "gy", [(i, (i + k) % n_y) for i in range(n_y)])

    def shift_chip(a, k):
        return lax.ppermute(a, "gz", [(i, (i + 2 * k) % n_z) for i in range(n_z)])

    def swap_core(a):
        return lax.ppermute(a, "gz", [(i, i ^ 1) for i in range(n_z)])

    def groups(a):
        return [shift_y(a, k) for k in range(1, n_y)]

    def chips(a):
        return [shift_chip(a, k) for k in range(1, n_z // 2)]

    def sum_blocks(parts, n):
        rows = parts[0].shape[0] // n
        sums = []
        for k in range(n):
            cut = [part[k * rows : (k + 1) * rows].astype(f32) for part in parts]
            sums.append(sum(cut[1:], cut[0]))
        return sums[:1] + [a.astype(bf16) for a in sums[1:]]

    def exchange(parts, shift):
        return parts[:1] + [shift(part, -k) for k, part in enumerate(parts) if k]

    def sum_width(part):
        part = part.astype(bf16).reshape(n_x, part.shape[0] // n_x, part.shape[1])
        parts = lax.all_to_all(part, "gx", 0, 0, tiled=True)
        return jnp.sum(parts.astype(f32), axis=0)

    def copies(share):
        return jnp.broadcast_to(share[None], (n_x, *share.shape))

    def gather_width(share_copies):
        parts = lax.all_to_all(share_copies, "gx", 0, 0, tiled=True)
        return parts.reshape(-1, parts.shape[-1])

    def after(a, *others):
        return lax.optimization_barrier((a, *others))[0]

    def shards(tokens, weight_in, bias_hidden, weight_out, grad_output):
        n_chip = n_z // 2
        rows = tokens.shape[0]
        tokens_groups, grad_chips = lax.optimization_barrier((groups(tokens), chips(grad_output)))
        tokens_far = jnp.concatenate([tokens] + tokens_groups, axis=0)
        grad_far = jnp.concatenate([grad_output] + grad_chips, axis=0)
        tokens_chips = chips(tokens_far)
        middle = n_y // 2
        grad_groups = {k: shift_y(grad_far, k) for k in range(1, n_y) if k != middle}
        tokens_chips, grad_groups = lax.optimization_barrier((tokens_chips, grad_groups))
        tokens_near = jnp.concatenate([tokens_far] + tokens_chips, axis=0)
        tokens_all = jnp.concatenate([tokens_near, swap_core(tokens_near)], axis=0)
        total_rows = tokens_all.shape[0]
        half = total_rows // 2
        norm_scale = 1.0 / math.sqrt(total_rows)
        pre_part = jnp.dot(tokens_all, weight_in, preferred_element_type=f32).astype(bf16)
        pre_act = sum_width(pre_part) + bias_hidden
        first = (n_chip - 1) * rows
        grad_groups[middle] = jnp.concatenate(
            [shift_y(grad_far[:first], middle), shift_y(after(grad_far[first:], pre_part), middle)],
            axis=0,
        )
        grad_near = jnp.stack(
            [
                a.reshape(n_chip, rows, a.shape[1])
                for a in [grad_far] + [grad_groups[k] for k in range(1, n_y)]
            ],
            axis=1,
        ).reshape(-1, grad_far.shape[1])
        grad_all = jnp.concatenate([grad_near, swap_core(grad_near)], axis=0)
        upstream = sum_width(contract_last(grad_all, weight_out))
        act_share, grad_share = gelu_pair(pre_act, upstream)
        grad_hidden = gather_width(copies(grad_share))
        other = contract_last(grad_hidden[half:], weight_in).astype(bf16)
        other, act_copies = lax.optimization_barrier((other, copies(act_share)))
        activation = gather_width(act_copies)
        own = contract_last(grad_hidden[:half], weight_in)
        own, other = lax.optimization_barrier((own, swap_core(other)))
        parts, beside = lax.optimization_barrier((sum_blocks([own, other], n_chip), grad_hidden))
        parts = exchange(parts, shift_chip)
        grad_weight_in = (contract_first(tokens_all, beside) * norm_scale).astype(bf16)
        parts, grad_weight_in = lax.optimization_barrier((parts, grad_weight_in))
        parts = exchange(sum_blocks(parts, n_y), shift_y)
        grad_weight_out = (contract_first(activation, grad_all) * norm_scale).astype(bf16)
        parts, grad_weight_out = lax.optimization_barrier((parts, grad_weight_out))
        (grad_tokens,) = sum_blocks(parts, 1)
        return (grad_tokens.astype(bf16), grad_weight_in, grad_weight_out)

    return jax.shard_map(
        shards,
        mesh=mesh,
        in_specs=(
            P(("gy", "gz"), "gx"),
            P("gx", ("gy", "gz")),
            P(("gy", "gz")),
            P(("gy", "gz"), "gx"),
            P(("gy", "gz"), "gx"),
        ),
        out_specs=(P(("gy", "gz"), "gx"), P("gx", ("gy", "gz")), P(("gy", "gz"), "gx")),
        check_vma=False,
    )
```

```python
import math

import jax
import jax.numpy as jnp
from jax import lax
from jax.sharding import PartitionSpec as P

root_coef = math.sqrt(2.0 / math.pi)
cubic_coef = 0.044715
bf16 = jnp.bfloat16
f32 = jnp.float32


def gelu_pair(pre_act, upstream):
    tanh_part = jnp.tanh(root_coef * (pre_act + cubic_coef * pre_act * pre_act * pre_act))
    activation = 0.5 * pre_act * (1.0 + tanh_part)
    slope_value = 0.5 * (1.0 + tanh_part) + 0.5 * pre_act * (
        1.0 - tanh_part * tanh_part
    ) * root_coef * (1.0 + 3.0 * cubic_coef * pre_act * pre_act)
    return (activation.astype(bf16), (upstream * slope_value).astype(bf16))


def contract_last(left, right):
    return lax.dot_general(left, right, (((1,), (1,)), ((), ())), preferred_element_type=f32)


def contract_first(left, right):
    return lax.dot_general(left, right, (((0,), (0,)), ((), ())), preferred_element_type=f32)


def solution(mesh):
    n_x, n_y, n_z = (mesh.shape[a] for a in ("gx", "gy", "gz"))

    def shift_y(a, k):
        return lax.ppermute(a, "gy", [(i, (i + k) % n_y) for i in range(n_y)])

    def shift_chip(a, k):
        return lax.ppermute(a, "gz", [(i, (i + 2 * k) % n_z) for i in range(n_z)])

    def swap_core(a):
        return lax.ppermute(a, "gz", [(i, i ^ 1) for i in range(n_z)])

    n_chip = n_z // 2

    def groups(a):
        return [a] + [shift_y(a, k) for k in range(1, n_y)]

    def sum_blocks(parts, n):
        rows = parts[0].shape[0] // n
        sums = []
        for k in range(n):
            cut = [part[k * rows : (k + 1) * rows].astype(f32) for part in parts]
            sums.append(sum(cut[1:], cut[0]))
        return sums[:1] + [a.astype(bf16) for a in sums[1:]]

    def exchange(parts, shift):
        return parts[:1] + [shift(part, -k) for k, part in enumerate(parts) if k]

    def copies(share):
        return jnp.broadcast_to(share[None], (n_x, *share.shape))

    def trade_width(parts):
        return lax.all_to_all(parts, "gx", 0, 0, tiled=True)

    def after(a, *others):
        return lax.optimization_barrier((a, *others))[0]

    def join(parts):
        return jnp.concatenate(parts, axis=1)

    def barrier(*values):
        return lax.optimization_barrier(values)

    def shards(tokens, weight_in, bias_hidden, weight_out, grad_output):
        norm_scale = 1.0 / math.sqrt(tokens.shape[0] * n_y * n_z)
        rows = tokens.shape[0] // 2
        chunks = [
            jnp.stack([a[c * rows : (c + 1) * rows] for a in (tokens, grad_output)]) for c in range(2)
        ]

        def partial_sums(near):
            both = [jnp.concatenate([a, swap_core(a)], axis=0) for a in near]
            pre_part = jnp.dot(both[0], weight_in, preferred_element_type=f32).astype(bf16)
            up_part = contract_last(both[1], weight_out).astype(bf16)
            parts = [a.reshape(n_x, 1, -1, a.shape[1]) for a in (pre_part, up_part)]
            return both, jnp.concatenate(parts, axis=1)

        def hidden(parts):
            sums = jnp.sum(parts.astype(f32), axis=0)
            return gelu_pair(sums[0] + bias_hidden, sums[1])

        far0 = join(groups(chunks[0]))
        groups1 = groups(after(chunks[1], far0))
        chips0, groups1 = barrier([far0] + [shift_chip(far0, k) for k in range(1, n_chip)], groups1)
        far1 = join(groups1)
        both0, part0 = partial_sums(join(chips0))
        last = n_chip // 2
        chips1 = [far1] + [
            shift_chip(after(far1, part0) if k == last else far1, k) for k in range(1, n_chip)
        ]
        both1, part1 = partial_sums(join(chips1))
        sums0 = trade_width(part0)
        sums1 = trade_width(part1)
        act0, grad0 = hidden(sums0)
        copies0, sums1 = barrier(copies(grad0), sums1)
        act1, grad1 = hidden(sums1)
        act_copies = copies(jnp.stack([act0, act1]))

        def two_halves(grad_hidden):
            half = grad_hidden.shape[0] // 2
            other = contract_last(grad_hidden[half:], weight_in).astype(bf16)
            return other, contract_last(grad_hidden[:half], weight_in)

        hidden0 = trade_width(copies0).reshape(-1, act0.shape[1])
        hidden1 = trade_width(after(copies(grad1), hidden0)).reshape(-1, act0.shape[1])
        other0, own0 = two_halves(hidden0)
        own0, other0 = barrier(own0, swap_core(other0))
        parts0 = exchange(sum_blocks([own0, other0], n_chip), shift_chip)
        other1, own1 = two_halves(hidden1)
        parts0, other1, act_copies = barrier(parts0, other1, act_copies)
        activation = trade_width(act_copies)
        own1, other1 = barrier(own1, swap_core(other1))
        parts1, beside = barrier(
            sum_blocks([own1, other1], n_chip), jnp.concatenate([hidden0, hidden1], axis=0)
        )
        parts1 = exchange(parts1, shift_chip)
        parts0 = exchange(sum_blocks(parts0, n_y), shift_y)
        tokens_all = jnp.concatenate([both0[0], both1[0]], axis=0)
        grad_weight_in = (contract_first(tokens_all, beside) * norm_scale).astype(bf16)
        parts0, parts1, grad_weight_in = barrier(parts0, parts1, grad_weight_in)
        parts1 = exchange(sum_blocks(parts1, n_y), shift_y)
        (tokens0,) = sum_blocks(parts0, 1)
        activation = activation.transpose(1, 0, 2, 3).reshape(-1, act0.shape[1])
        grad_all = jnp.concatenate([both0[1], both1[1]], axis=0)
        grad_weight_out = (contract_first(activation, grad_all) * norm_scale).astype(bf16)
        parts1, grad_weight_out = barrier(parts1, grad_weight_out)
        (tokens1,) = sum_blocks(parts1, 1)
        grad_tokens = jnp.concatenate([tokens0, tokens1], axis=0).astype(bf16)
        return (grad_tokens, grad_weight_in, grad_weight_out)

    return jax.shard_map(
        shards,
        mesh=mesh,
        in_specs=(
            P(("gy", "gz"), "gx"),
            P("gx", ("gy", "gz")),
            P(("gy", "gz")),
            P(("gy", "gz"), "gx"),
            P(("gy", "gz"), "gx"),
        ),
        out_specs=(P(("gy", "gz"), "gx"), P("gx", ("gy", "gz")), P(("gy", "gz"), "gx")),
        check_vma=False,
    )
```

```python
import math

import jax
import jax.numpy as jnp
from jax import lax
from jax.sharding import PartitionSpec as P

root_coef = math.sqrt(2.0 / math.pi)
cubic_coef = 0.044715
bf16 = jnp.bfloat16
f32 = jnp.float32


def gelu_pair(pre_act, upstream):
    tanh_part = jnp.tanh(root_coef * (pre_act + cubic_coef * pre_act * pre_act * pre_act))
    activation = 0.5 * pre_act * (1.0 + tanh_part)
    slope_value = 0.5 * (1.0 + tanh_part) + 0.5 * pre_act * (
        1.0 - tanh_part * tanh_part
    ) * root_coef * (1.0 + 3.0 * cubic_coef * pre_act * pre_act)
    return (activation.astype(bf16), (upstream * slope_value).astype(bf16))


def contract_last(left, right):
    return lax.dot_general(left, right, (((1,), (1,)), ((), ())), preferred_element_type=f32)


def contract_first(left, right):
    return lax.dot_general(left, right, (((0,), (0,)), ((), ())), preferred_element_type=f32)


def solution(mesh):
    n_x, n_y, n_z = (mesh.shape[a] for a in ("gx", "gy", "gz"))

    def shift_y(a, k):
        return lax.ppermute(a, "gy", [(i, (i + k) % n_y) for i in range(n_y)])

    def shift_chip(a, k):
        return lax.ppermute(a, "gz", [(i, (i + 2 * k) % n_z) for i in range(n_z)])

    def swap_core(a):
        return lax.ppermute(a, "gz", [(i, i ^ 1) for i in range(n_z)])

    n_chip = n_z // 2

    def groups(a):
        return [a] + [shift_y(a, k) for k in range(1, n_y)]

    def sum_blocks(parts, n):
        rows = parts[0].shape[0] // n
        sums = []
        for k in range(n):
            cut = [part[k * rows : (k + 1) * rows].astype(f32) for part in parts]
            sums.append(sum(cut[1:], cut[0]))
        return sums[:1] + [a.astype(bf16) for a in sums[1:]]

    def exchange(parts, shift):
        return parts[:1] + [shift(part, -k) for k, part in enumerate(parts) if k]

    def copies(share):
        return jnp.broadcast_to(share[None], (n_x, *share.shape))

    def trade_width(parts):
        return lax.all_to_all(parts, "gx", 0, 0, tiled=True)

    def after(a, *others):
        return lax.optimization_barrier((a, *others))[0]

    def join(parts):
        return jnp.concatenate(parts, axis=1)

    def barrier(*values):
        return lax.optimization_barrier(values)

    def shards(tokens, weight_in, bias_hidden, weight_out, grad_output):
        norm_scale = 1.0 / math.sqrt(tokens.shape[0] * n_y * n_z)
        rows = tokens.shape[0] // 2
        chunks = [
            jnp.stack([a[c * rows : (c + 1) * rows] for a in (tokens, grad_output)]) for c in range(2)
        ]

        def partial_sums(near):
            both = [jnp.concatenate([a, swap_core(a)], axis=0) for a in near]
            pre_part = jnp.dot(both[0], weight_in, preferred_element_type=f32).astype(bf16)
            up_part = contract_last(both[1], weight_out).astype(bf16)
            parts = [a.reshape(n_x, 1, -1, a.shape[1]) for a in (pre_part, up_part)]
            return both, jnp.concatenate(parts, axis=1)

        def hidden(parts):
            sums = jnp.sum(parts.astype(f32), axis=0)
            return gelu_pair(sums[0] + bias_hidden, sums[1])

        far0 = join(groups(chunks[0]))
        groups1 = groups(after(chunks[1], far0))
        chips0, groups1 = barrier([far0] + [shift_chip(far0, k) for k in range(1, n_chip)], groups1)
        far1 = join(groups1)
        both0, part0 = partial_sums(join(chips0))
        chips1 = [far1] + [
            shift_chip(far1, k) for k in range(1, n_chip)
        ]
        both1, part1 = partial_sums(join(chips1))
        sums0 = trade_width(part0)
        sums1 = trade_width(part1)
        act0, grad0 = hidden(sums0)
        copies0, sums1 = barrier(copies(grad0), sums1)
        act1, grad1 = hidden(sums1)
        act_copies = copies(jnp.stack([act0, act1]))

        def two_halves(grad_hidden):
            half = grad_hidden.shape[0] // 2
            other = contract_last(grad_hidden[half:], weight_in).astype(bf16)
            return other, contract_last(grad_hidden[:half], weight_in)

        hidden0 = trade_width(copies0).reshape(-1, act0.shape[1])
        hidden1 = trade_width(after(copies(grad1), hidden0)).reshape(-1, act0.shape[1])
        other0, own0 = two_halves(hidden0)
        own0, other0 = barrier(own0, swap_core(other0))
        parts0, act_copies = barrier(sum_blocks([own0, other0], n_chip), act_copies)
        parts0 = exchange(parts0, shift_chip)
        other1, own1 = two_halves(hidden1)
        parts0, other1, act_copies = barrier(parts0, other1, act_copies)
        activation = trade_width(act_copies)
        own1, other1 = barrier(own1, swap_core(other1))
        parts1, hidden0, hidden1 = barrier(sum_blocks([own1, other1], n_chip), hidden0, hidden1)
        parts1 = exchange(parts1, shift_chip)
        hidden_all = jnp.concatenate([hidden0, hidden1], axis=0)
        tokens_all = jnp.concatenate([both0[0], both1[0]], axis=0)
        grad_weight_in = (contract_first(tokens_all, hidden_all) * norm_scale).astype(bf16)
        parts0, parts1, grad_weight_in = barrier(parts0, parts1, grad_weight_in)
        parts = [
            jnp.concatenate(pair, axis=0)
            for pair in zip(sum_blocks(parts0, n_y), sum_blocks(parts1, n_y))
        ]
        parts = exchange(parts, shift_y)
        activation = activation.transpose(1, 0, 2, 3).reshape(-1, act0.shape[1])
        grad_all = jnp.concatenate([both0[1], both1[1]], axis=0)
        grad_weight_out = (contract_first(activation, grad_all) * norm_scale).astype(bf16)
        parts, grad_weight_out = barrier(parts, grad_weight_out)
        (grad_tokens,) = sum_blocks(parts, 1)
        return (grad_tokens.astype(bf16), grad_weight_in, grad_weight_out)

    return jax.shard_map(
        shards,
        mesh=mesh,
        in_specs=(
            P(("gy", "gz"), "gx"),
            P("gx", ("gy", "gz")),
            P(("gy", "gz")),
            P(("gy", "gz"), "gx"),
            P(("gy", "gz"), "gx"),
        ),
        out_specs=(P(("gy", "gz"), "gx"), P("gx", ("gy", "gz")), P(("gy", "gz"), "gx")),
        check_vma=False,
    )
```

```python
import math

import jax
import jax.numpy as jnp
from jax import lax
from jax.experimental import pallas as pl
from jax.experimental.pallas import tpu as pltpu
from jax.sharding import PartitionSpec as P

root_coef = math.sqrt(2.0 / math.pi)
cubic_coef = 0.044715
bf16 = jnp.bfloat16
f32 = jnp.float32


def gelu_pair(pre_act, upstream):
    tanh_part = jnp.tanh(root_coef * (pre_act + cubic_coef * pre_act * pre_act * pre_act))
    activation = 0.5 * pre_act * (1.0 + tanh_part)
    slope_value = 0.5 * (1.0 + tanh_part) + 0.5 * pre_act * (
        1.0 - tanh_part * tanh_part
    ) * root_coef * (1.0 + 3.0 * cubic_coef * pre_act * pre_act)
    return (activation.astype(bf16), (upstream * slope_value).astype(bf16))


def contract_last(left, right):
    return lax.dot_general(left, right, (((1,), (1,)), ((), ())), preferred_element_type=f32)


def contract_first(left, right):
    return lax.dot_general(left, right, (((0,), (0,)), ((), ())), preferred_element_type=f32)


def vmem(mib):
    return pltpu.CompilerParams(vmem_limit_bytes=mib << 20)


def hidden_kernel(parts, bias, *refs):
    before, (grad_copies, act_out) = refs[:-2], refs[-2:]
    sums = jnp.sum(parts[...].astype(f32), axis=0)
    act, grad = gelu_pair(sums[0] + bias[...], sums[1])
    grad_copies[...] = jnp.broadcast_to(grad[None], grad_copies.shape)
    if before:
        act_out[:, 0] = jnp.broadcast_to(before[0][...][None], grad_copies.shape)
        act_out[:, 1] = jnp.broadcast_to(act[None], grad_copies.shape)
    else:
        act_out[...] = act


def hidden(parts, bias, *before):
    n, pair, rows, columns = parts.shape
    tile = columns // 3
    act_shape = (n, 2, rows) if before else (rows,)
    return pl.pallas_call(
        hidden_kernel,
        grid=(columns // tile,),
        in_specs=[
            pl.BlockSpec((n, pair, rows, tile), lambda i: (0, 0, 0, i)),
            pl.BlockSpec((1, tile), lambda i: (0, i)),
        ]
        + [pl.BlockSpec((rows, tile), lambda i: (0, i))] * len(before),
        out_specs=[
            pl.BlockSpec((n, rows, tile), lambda i: (0, 0, i)),
            pl.BlockSpec((*act_shape, tile), lambda i: (*([0] * len(act_shape)), i)),
        ],
        out_shape=[
            jax.ShapeDtypeStruct((n, rows, columns), bf16),
            jax.ShapeDtypeStruct((*act_shape, columns), bf16),
        ],
        compiler_params=vmem(32),
        cost_estimate=pl.CostEstimate(
            flops=40 * rows * columns,
            bytes_accessed=2 * (parts.size + n * rows * columns),
            transcendentals=rows * columns,
        ),
    )(parts, bias, *before)


def times_weight(hidden_ref, weight_ref):
    return lax.dot_general(
        hidden_ref[...], weight_ref[...], (((1,), (1,)), ((), ())), preferred_element_type=f32
    )


def other_kernel(hidden_ref, weight_ref, out_ref):
    out_ref[...] = times_weight(hidden_ref, weight_ref).astype(bf16)


def own_kernel(hidden_ref, weight_ref, received_ref, *out_refs):
    total = times_weight(hidden_ref, weight_ref) + received_ref[...].astype(f32)
    rows = out_refs[0].shape[0]
    for k, out_ref in enumerate(out_refs):
        out_ref[...] = total[k * rows : (k + 1) * rows].astype(out_ref.dtype)


def half_times_weight(kernel, place, grad_hidden, weight_in, received, out_shape):
    half, depth = grad_hidden.shape[0] // 2, grad_hidden.shape[1]
    width = weight_in.shape[0]
    tile = width // 3
    return pl.pallas_call(
        kernel,
        grid=(width // tile,),
        in_specs=[
            pl.BlockSpec((half, depth), lambda i: (place, 0)),
            pl.BlockSpec((tile, depth), lambda i: (i, 0)),
        ]
        + [pl.BlockSpec((half, tile), lambda i: (0, i))] * len(received),
        out_specs=[pl.BlockSpec((a.shape[0], tile), lambda i: (0, i)) for a in out_shape],
        out_shape=out_shape,
        compiler_params=vmem(32),
        cost_estimate=pl.CostEstimate(
            flops=2 * half * depth * width,
            bytes_accessed=2 * (half * depth + depth * width + 2 * half * width),
            transcendentals=0,
        ),
    )(grad_hidden, weight_in, *received)


def solution(mesh):
    n_x, n_y, n_z = (mesh.shape[a] for a in ("gx", "gy", "gz"))

    def shift_y(a, k):
        return lax.ppermute(a, "gy", [(i, (i + k) % n_y) for i in range(n_y)])

    def shift_chip(a, k):
        return lax.ppermute(a, "gz", [(i, (i + 2 * k) % n_z) for i in range(n_z)])

    def swap_core(a):
        return lax.ppermute(a, "gz", [(i, i ^ 1) for i in range(n_z)])

    n_chip = n_z // 2

    def groups(a):
        return [a] + [shift_y(a, k) for k in range(1, n_y)]

    def sum_blocks(parts, n):
        rows = parts[0].shape[0] // n
        sums = []
        for k in range(n):
            cut = [part[k * rows : (k + 1) * rows].astype(f32) for part in parts]
            sums.append(sum(cut[1:], cut[0]))
        return sums[:1] + [a.astype(bf16) for a in sums[1:]]

    def exchange(parts, shift):
        return [shift(part, -k) if k else part for k, part in enumerate(parts)]

    def trade_width(parts):
        return lax.all_to_all(parts, "gx", 0, 0, tiled=True)

    def after(a, *others):
        return lax.optimization_barrier((a, *others))[0]

    def join(parts):
        return jnp.concatenate(parts, axis=1)

    def barrier(*values):
        return lax.optimization_barrier(values)

    def shards(tokens, weight_in, bias_hidden, weight_out, grad_output):
        norm_scale = 1.0 / math.sqrt(tokens.shape[0] * n_y * n_z)
        rows = tokens.shape[0] // 2
        chunks = [
            jnp.stack([a[c * rows : (c + 1) * rows] for a in (tokens, grad_output)]) for c in range(2)
        ]
        bias = bias_hidden.reshape(1, -1)

        def partial_sums(pieces):
            both = [jnp.concatenate([a, swap_core(a)], axis=0) for a in join(pieces)]
            pre_part = jnp.dot(both[0], weight_in, preferred_element_type=f32).astype(bf16)
            up_part = contract_last(both[1], weight_out).astype(bf16)
            parts = [a.reshape(n_x, 1, -1, a.shape[1]) for a in (pre_part, up_part)]
            return both, jnp.concatenate(parts, axis=1)

        def other_rows(grad_hidden):
            shape = jax.ShapeDtypeStruct((grad_hidden.shape[0] // 2, weight_in.shape[0]), bf16)
            return half_times_weight(other_kernel, 1, grad_hidden, weight_in, [], [shape])[0]

        def own_rows(grad_hidden, received):
            shape = (received.shape[0] // n_chip, received.shape[1])
            shapes = [jax.ShapeDtypeStruct(shape, bf16 if k else f32) for k in range(n_chip)]
            return half_times_weight(own_kernel, 0, grad_hidden, weight_in, [received], shapes)

        far0 = join(groups(chunks[0]))
        far1 = join(groups(after(chunks[1], far0)))
        chips0, far1 = barrier([far0] + [shift_chip(far0, k) for k in range(1, n_chip)], far1)
        both0, part0 = partial_sums(chips0)
        both1, part1 = partial_sums([far1] + [shift_chip(far1, k) for k in range(1, n_chip)])
        sums0 = trade_width(part0)
        sums1 = trade_width(part1)
        grad_copies0, act0 = hidden(sums0, bias)
        grad_copies0, sums1 = barrier(grad_copies0, sums1)
        grad_copies1, act_copies = hidden(sums1, bias, act0)
        columns = act0.shape[1]
        hidden0 = trade_width(grad_copies0)
        hidden0, grad_copies1 = barrier(hidden0, grad_copies1)
        hidden1 = trade_width(grad_copies1).reshape(-1, columns)
        hidden0 = hidden0.reshape(-1, columns)
        parts0 = own_rows(hidden0, swap_core(other_rows(hidden0)))
        parts0 = exchange(parts0, shift_chip)
        other1 = other_rows(hidden1)
        parts0[: n_chip - 1], other1, act_copies = barrier(parts0[: n_chip - 1], other1, act_copies)
        activation = trade_width(act_copies)
        parts1 = own_rows(hidden1, swap_core(other1))
        parts0, parts1, hidden0, hidden1 = barrier(parts0, parts1, hidden0, hidden1)
        parts1 = exchange(parts1, shift_chip)
        hidden_all = jnp.concatenate([hidden0, hidden1], axis=0)
        tokens_all = jnp.concatenate([both0[0], both1[0]], axis=0)
        grad_weight_in = (contract_first(tokens_all, hidden_all) * norm_scale).astype(bf16)
        parts0, parts1, grad_weight_in = barrier(parts0, parts1, grad_weight_in)
        parts = [
            jnp.concatenate(pair, axis=0)
            for pair in zip(sum_blocks(parts0, n_y), sum_blocks(parts1, n_y))
        ]
        parts = exchange(parts, shift_y)
        activation = activation.transpose(1, 0, 2, 3).reshape(-1, columns)
        grad_all = jnp.concatenate([both0[1], both1[1]], axis=0)
        grad_weight_out = (contract_first(activation, grad_all) * norm_scale).astype(bf16)
        parts, grad_weight_out = barrier(parts, grad_weight_out)
        (grad_tokens,) = sum_blocks(parts, 1)
        return (grad_tokens.astype(bf16), grad_weight_in, grad_weight_out)

    return jax.shard_map(
        shards,
        mesh=mesh,
        in_specs=(
            P(("gy", "gz"), "gx"),
            P("gx", ("gy", "gz")),
            P(("gy", "gz")),
            P(("gy", "gz"), "gx"),
            P(("gy", "gz"), "gx"),
        ),
        out_specs=(P(("gy", "gz"), "gx"), P("gx", ("gy", "gz")), P(("gy", "gz"), "gx")),
        check_vma=False,
    )
```

```python
import functools
import math

import jax
import jax.numpy as jnp
from jax import lax
from jax.experimental import pallas as pl
from jax.experimental.pallas import tpu as pltpu
from jax.sharding import PartitionSpec as P

root_coef = math.sqrt(2.0 / math.pi)
cubic_coef = 0.044715
bf16 = jnp.bfloat16
f32 = jnp.float32


def gelu_pair(pre_act, upstream):
    tanh_part = jnp.tanh(root_coef * (pre_act + cubic_coef * pre_act * pre_act * pre_act))
    activation = 0.5 * pre_act * (1.0 + tanh_part)
    slope_value = 0.5 * (1.0 + tanh_part) + 0.5 * pre_act * (
        1.0 - tanh_part * tanh_part
    ) * root_coef * (1.0 + 3.0 * cubic_coef * pre_act * pre_act)
    return (activation.astype(bf16), (upstream * slope_value).astype(bf16))


def contract_last(left, right):
    return lax.dot_general(left, right, (((1,), (1,)), ((), ())), preferred_element_type=f32)


def contract_first(left, right):
    return lax.dot_general(left, right, (((0,), (0,)), ((), ())), preferred_element_type=f32)


def vmem(mib):
    return pltpu.CompilerParams(vmem_limit_bytes=mib << 20)


def hidden_kernel(n_parts, n_copies, bias, *refs):
    parts, before, (grad_copies, act_out) = refs[:n_parts], refs[n_parts:-2], refs[-2:]
    blocks = [ref[j] for ref in parts for j in range(ref.shape[0])]
    sums = blocks[0].astype(f32)
    for block in blocks[1:]:
        sums = sums + block.astype(f32)
    act, grad = gelu_pair(sums[0] + bias[...], sums[1])
    for j in range(n_copies):
        grad_copies[j] = grad
        if before:
            act_out[j, 0] = before[0][...]
            act_out[j, 1] = act
    if not before:
        act_out[...] = act


def hidden(parts, n_copies, bias, *before):
    pair, rows, columns = parts[0].shape[1:]
    tile = columns // 3
    act_shape = (n_copies, 2, rows) if before else (rows,)
    return pl.pallas_call(
        functools.partial(hidden_kernel, len(parts), n_copies),
        grid=(columns // tile,),
        in_specs=[pl.BlockSpec((1, tile), lambda i: (0, i))]
        + [pl.BlockSpec((a.shape[0], pair, rows, tile), lambda i: (0, 0, 0, i)) for a in parts]
        + [pl.BlockSpec((rows, tile), lambda i: (0, i))] * len(before),
        out_specs=[
            pl.BlockSpec((n_copies, rows, tile), lambda i: (0, 0, i)),
            pl.BlockSpec((*act_shape, tile), lambda i: (*([0] * len(act_shape)), i)),
        ],
        out_shape=[
            jax.ShapeDtypeStruct((n_copies, rows, columns), bf16),
            jax.ShapeDtypeStruct((*act_shape, columns), bf16),
        ],
        compiler_params=pltpu.CompilerParams(vmem_limit_bytes=32 << 20),
        cost_estimate=pl.CostEstimate(
            flops=40 * rows * columns,
            bytes_accessed=6 * n_copies * rows * columns,
            transcendentals=rows * columns,
        ),
    )(bias, *parts, *before)


def solution(mesh):
    n_x, n_y, n_z = (mesh.shape[a] for a in ("gx", "gy", "gz"))

    def shift_y(a, k):
        return lax.ppermute(a, "gy", [(i, (i + k) % n_y) for i in range(n_y)])

    def shift_chip(a, k):
        return lax.ppermute(a, "gz", [(i, (i + 2 * k) % n_z) for i in range(n_z)])

    def swap_core(a):
        return lax.ppermute(a, "gz", [(i, i ^ 1) for i in range(n_z)])

    n_chip = n_z // 2

    def groups(a):
        return [a] + [shift_y(a, k) for k in range(1, n_y)]

    def sum_blocks(parts, n):
        rows = parts[0].shape[0] // n
        sums = []
        for k in range(n):
            cut = [part[k * rows : (k + 1) * rows].astype(f32) for part in parts]
            sums.append(sum(cut[1:], cut[0]))
        return sums[:1] + [a.astype(bf16) for a in sums[1:]]

    def exchange(parts, shift):
        return [shift(part, -k) if k else part for k, part in enumerate(parts)]

    def trade_width(parts):
        return lax.all_to_all(parts, "gx", 0, 0, tiled=True)

    def permute_width(parts):
        place = lax.axis_index("gx").astype(jnp.uint32)
        received = []
        for flip in sorted(range(n_x), key=lambda flip: -(flip // (n_x // 2) + (flip % (n_x // 2)) % 3)):
            block = lax.dynamic_slice_in_dim(parts, place ^ flip, 1, axis=0)
            if flip:
                block = lax.ppermute(block, "gx", [(i, i ^ flip) for i in range(n_x)])
            received.append(block)
        return received

    def after(a, *others):
        return lax.optimization_barrier((a, *others))[0]

    def join(parts):
        return jnp.concatenate(parts, axis=1)

    def barrier(*values):
        return lax.optimization_barrier(values)

    def shards(tokens, weight_in, bias_hidden, weight_out, grad_output):
        norm_scale = 1.0 / math.sqrt(tokens.shape[0] * n_y * n_z)
        rows = tokens.shape[0] // 2
        chunks = [
            jnp.stack([a[c * rows : (c + 1) * rows] for a in (tokens, grad_output)]) for c in range(2)
        ]
        bias = bias_hidden.reshape(1, -1)

        def partial_sums(pieces):
            both = [jnp.concatenate([a, swap_core(a)], axis=0) for a in join(pieces)]
            pre_part = jnp.dot(both[0], weight_in, preferred_element_type=f32).astype(bf16)
            up_part = contract_last(both[1], weight_out).astype(bf16)
            parts = [a.reshape(n_x, 1, -1, a.shape[1]) for a in (pre_part, up_part)]
            return both, jnp.concatenate(parts, axis=1)

        def two_halves(grad_hidden):
            half = grad_hidden.shape[0] // 2
            other = contract_last(grad_hidden[half:], weight_in).astype(bf16)
            return other, contract_last(grad_hidden[:half], weight_in)

        far0 = join(groups(chunks[0]))
        far1 = join(groups(after(chunks[1], far0)))
        chips0, far1 = barrier([far0] + [shift_chip(far0, k) for k in range(1, n_chip)], far1)
        both0, part0 = partial_sums(chips0)
        both1, part1 = partial_sums([far1] + [shift_chip(far1, k) for k in range(1, n_chip)])
        sums0 = trade_width(part0)
        sums0, part1 = barrier(sums0, part1)
        sums1 = permute_width(part1)
        grad_copies0, act0 = hidden([sums0], n_x, bias)
        columns = act0.shape[1]
        hidden0 = trade_width(grad_copies0)
        hidden0, sums1 = barrier(hidden0, sums1)
        grad_copies1, act_copies = hidden(sums1, n_x, bias, act0)
        hidden1 = trade_width(grad_copies1).reshape(-1, columns)
        hidden0 = hidden0.reshape(-1, columns)
        other0, own0 = two_halves(hidden0)
        own0, other0 = barrier(own0, swap_core(other0))
        parts0 = exchange(sum_blocks([own0, other0], n_chip), shift_chip)
        other1, own1 = two_halves(hidden1)
        parts0, other1, act_copies = barrier(parts0, other1, act_copies)
        activation = trade_width(act_copies)
        own1, other1 = barrier(own1, swap_core(other1))
        parts1, hidden0, hidden1 = barrier(sum_blocks([own1, other1], n_chip), hidden0, hidden1)
        parts1 = exchange(parts1, shift_chip)
        hidden_all = jnp.concatenate([hidden0, hidden1], axis=0)
        tokens_all = jnp.concatenate([both0[0], both1[0]], axis=0)
        grad_weight_in = (contract_first(tokens_all, hidden_all) * norm_scale).astype(bf16)
        parts0, parts1, grad_weight_in = barrier(parts0, parts1, grad_weight_in)
        parts = [
            jnp.concatenate(pair, axis=0)
            for pair in zip(sum_blocks(parts0, n_y), sum_blocks(parts1, n_y))
        ]
        parts = exchange(parts, shift_y)
        activation = activation.transpose(1, 0, 2, 3).reshape(-1, columns)
        grad_all = jnp.concatenate([both0[1], both1[1]], axis=0)
        grad_weight_out = (contract_first(activation, grad_all) * norm_scale).astype(bf16)
        parts, grad_weight_out = barrier(parts, grad_weight_out)
        (grad_tokens,) = sum_blocks(parts, 1)
        return (grad_tokens.astype(bf16), grad_weight_in, grad_weight_out)

    return jax.shard_map(
        shards,
        mesh=mesh,
        in_specs=(
            P(("gy", "gz"), "gx"),
            P("gx", ("gy", "gz")),
            P(("gy", "gz")),
            P(("gy", "gz"), "gx"),
            P(("gy", "gz"), "gx"),
        ),
        out_specs=(P(("gy", "gz"), "gx"), P("gx", ("gy", "gz")), P(("gy", "gz"), "gx")),
        check_vma=False,
    )
```

```python
import functools
import math

import jax
import jax.numpy as jnp
from jax import lax
from jax.experimental import pallas as pl
from jax.experimental.pallas import tpu as pltpu
from jax.sharding import PartitionSpec as P

root_coef = math.sqrt(2.0 / math.pi)
cubic_coef = 0.044715
bf16 = jnp.bfloat16
f32 = jnp.float32


def gelu_pair(pre_act, upstream):
    tanh_part = jnp.tanh(root_coef * (pre_act + cubic_coef * pre_act * pre_act * pre_act))
    activation = 0.5 * pre_act * (1.0 + tanh_part)
    slope_value = 0.5 * (1.0 + tanh_part) + 0.5 * pre_act * (
        1.0 - tanh_part * tanh_part
    ) * root_coef * (1.0 + 3.0 * cubic_coef * pre_act * pre_act)
    return (activation.astype(bf16), (upstream * slope_value).astype(bf16))


def contract_last(left, right):
    return lax.dot_general(left, right, (((1,), (1,)), ((), ())), preferred_element_type=f32)


def contract_first(left, right):
    return lax.dot_general(left, right, (((0,), (0,)), ((), ())), preferred_element_type=f32)


def vmem(mib):
    return pltpu.CompilerParams(vmem_limit_bytes=mib << 20)


def hidden_kernel(parts, bias, *refs):
    before, (grad_copies, act_out) = refs[:-2], refs[-2:]
    sums = parts[0].astype(f32)
    for j in range(1, parts.shape[0]):
        sums = sums + parts[j].astype(f32)
    act, grad = gelu_pair(sums[0] + bias[...], sums[1])
    for j in range(parts.shape[0]):
        grad_copies[j] = grad
        if before:
            act_out[j, 0] = before[0][...]
            act_out[j, 1] = act
    if not before:
        act_out[...] = act


def hidden(parts, bias, *before):
    n, pair, rows, columns = parts.shape
    tile = columns // 3
    act_shape = (n, 2, rows) if before else (rows,)
    return pl.pallas_call(
        hidden_kernel,
        grid=(columns // tile,),
        in_specs=[
            pl.BlockSpec((n, pair, rows, tile), lambda i: (0, 0, 0, i)),
            pl.BlockSpec((1, tile), lambda i: (0, i)),
        ]
        + [pl.BlockSpec((rows, tile), lambda i: (0, i))] * len(before),
        out_specs=[
            pl.BlockSpec((n, rows, tile), lambda i: (0, 0, i)),
            pl.BlockSpec((*act_shape, tile), lambda i: (*([0] * len(act_shape)), i)),
        ],
        out_shape=[
            jax.ShapeDtypeStruct((n, rows, columns), bf16),
            jax.ShapeDtypeStruct((*act_shape, columns), bf16),
        ],
        compiler_params=pltpu.CompilerParams(vmem_limit_bytes=8 << 20),
        cost_estimate=pl.CostEstimate(
            flops=40 * rows * columns,
            bytes_accessed=6 * n * rows * columns,
            transcendentals=rows * columns,
        ),
    )(parts, bias, *before)


def join_kernel(n, *refs):
    ins, outs = refs[:-n], refs[-n:]
    chunk_rows = ins[0].shape[0] // n
    chunks = [ins[j : j + n] for j in range(0, len(ins), n)]
    for c, parts in enumerate(chunks):
        total = parts[0][...]
        for part in parts[1:]:
            total = total + part[...].astype(f32)
        for k, out in enumerate(outs):
            block = total[k * chunk_rows : (k + 1) * chunk_rows]
            out[c * chunk_rows : (c + 1) * chunk_rows] = block.astype(out.dtype)


def join_sums(chunks, n):
    rows, columns = chunks[0][0].shape
    tile = columns // 3
    out_rows = len(chunks) * rows // n
    ins = [part for parts in chunks for part in parts]
    return pl.pallas_call(
        functools.partial(join_kernel, n),
        grid=(columns // tile,),
        in_specs=[pl.BlockSpec((rows, tile), lambda i: (0, i))] * len(ins),
        out_specs=[pl.BlockSpec((out_rows, tile), lambda i: (0, i))] * n,
        out_shape=[
            jax.ShapeDtypeStruct((out_rows, columns), bf16 if k else f32) for k in range(n)
        ],
        compiler_params=pltpu.CompilerParams(vmem_limit_bytes=8 << 20),
        cost_estimate=pl.CostEstimate(
            flops=len(ins) * rows * columns,
            bytes_accessed=2 * len(ins) * rows * columns,
            transcendentals=0,
        ),
    )(*ins)


def solution(mesh):
    n_x, n_y, n_z = (mesh.shape[a] for a in ("gx", "gy", "gz"))

    def shift_y(a, k):
        return lax.ppermute(a, "gy", [(i, (i + k) % n_y) for i in range(n_y)])

    def shift_chip(a, k):
        return lax.ppermute(a, "gz", [(i, (i + 2 * k) % n_z) for i in range(n_z)])

    def swap_core(a):
        return lax.ppermute(a, "gz", [(i, i ^ 1) for i in range(n_z)])

    n_chip = n_z // 2

    def groups(a):
        return [a] + [shift_y(a, k) for k in range(1, n_y)]

    def sum_blocks(parts, n):
        rows = parts[0].shape[0] // n
        sums = []
        for k in range(n):
            cut = [part[k * rows : (k + 1) * rows].astype(f32) for part in parts]
            sums.append(sum(cut[1:], cut[0]))
        return sums[:1] + [a.astype(bf16) for a in sums[1:]]

    def exchange(parts, shift):
        return [shift(part, -k) if k else part for k, part in enumerate(parts)]

    def trade_width(parts):
        return lax.all_to_all(parts, "gx", 0, 0, tiled=True)

    def after(a, *others):
        return lax.optimization_barrier((a, *others))[0]

    def join(parts):
        return jnp.concatenate(parts, axis=1)

    def barrier(*values):
        return lax.optimization_barrier(values)

    def shards(tokens, weight_in, bias_hidden, weight_out, grad_output):
        norm_scale = 1.0 / math.sqrt(tokens.shape[0] * n_y * n_z)
        rows = tokens.shape[0] // 2
        chunks = [
            jnp.stack([a[c * rows : (c + 1) * rows] for a in (tokens, grad_output)]) for c in range(2)
        ]
        bias = bias_hidden.reshape(1, -1)

        def partial_sums(pieces):
            both = [jnp.concatenate([a, swap_core(a)], axis=0) for a in join(pieces)]
            pre_part = jnp.dot(both[0], weight_in, preferred_element_type=f32).astype(bf16)
            up_part = contract_last(both[1], weight_out).astype(bf16)
            parts = [a.reshape(n_x, 1, -1, a.shape[1]) for a in (pre_part, up_part)]
            return both, jnp.concatenate(parts, axis=1)

        def two_halves(grad_hidden):
            half = grad_hidden.shape[0] // 2
            other = contract_last(grad_hidden[half:], weight_in).astype(bf16)
            return other, contract_last(grad_hidden[:half], weight_in)

        far0 = join(groups(chunks[0]))
        far1 = join(groups(after(chunks[1], far0)))
        chips0, far1 = barrier([far0] + [shift_chip(far0, k) for k in range(1, n_chip)], far1)
        both0, part0 = partial_sums(chips0)
        both1, part1 = partial_sums([far1] + [shift_chip(far1, k) for k in range(1, n_chip)])
        sums0 = trade_width(part0)
        sums1 = trade_width(part1)
        grad_copies0, act0 = hidden(sums0, bias)
        columns = act0.shape[1]
        grad_copies0, sums1 = barrier(grad_copies0, sums1)
        hidden0 = trade_width(grad_copies0)
        grad_copies1, act_copies = hidden(sums1, bias, act0)
        hidden1 = trade_width(after(grad_copies1, hidden0)).reshape(-1, columns)
        hidden0 = hidden0.reshape(-1, columns)
        other0, own0 = two_halves(hidden0)
        own0, other0 = barrier(own0, swap_core(other0))
        parts0, act_copies = barrier(sum_blocks([own0, other0], n_chip), act_copies)
        parts0 = exchange(parts0, shift_chip)
        other1, own1 = two_halves(hidden1)
        parts0, other1, act_copies = barrier(parts0, other1, act_copies)
        activation = trade_width(act_copies)
        own1, other1 = barrier(own1, swap_core(other1))
        parts1, hidden0, hidden1 = barrier(sum_blocks([own1, other1], n_chip), hidden0, hidden1)
        parts1 = exchange(parts1, shift_chip)
        hidden_all = jnp.concatenate([hidden0, hidden1], axis=0)
        tokens_all = jnp.concatenate([both0[0], both1[0]], axis=0)
        grad_weight_in = (contract_first(tokens_all, hidden_all) * norm_scale).astype(bf16)
        parts0, parts1, grad_weight_in = barrier(parts0, parts1, grad_weight_in)
        parts = join_sums([parts0, parts1], n_y)
        parts = exchange(parts, shift_y)
        activation = activation.transpose(1, 0, 2, 3).reshape(-1, columns)
        grad_all = jnp.concatenate([both0[1], both1[1]], axis=0)
        grad_weight_out = (contract_first(activation, grad_all) * norm_scale).astype(bf16)
        parts, grad_weight_out = barrier(parts, grad_weight_out)
        (grad_tokens,) = sum_blocks(parts, 1)
        return (grad_tokens.astype(bf16), grad_weight_in, grad_weight_out)

    return jax.shard_map(
        shards,
        mesh=mesh,
        in_specs=(
            P(("gy", "gz"), "gx"),
            P("gx", ("gy", "gz")),
            P(("gy", "gz")),
            P(("gy", "gz"), "gx"),
            P(("gy", "gz"), "gx"),
        ),
        out_specs=(P(("gy", "gz"), "gx"), P("gx", ("gy", "gz")), P(("gy", "gz"), "gx")),
        check_vma=False,
    )
```

```python
import functools
import math

import jax
import jax.numpy as jnp
from jax import lax
from jax.experimental import pallas as pl
from jax.experimental.pallas import tpu as pltpu
from jax.sharding import PartitionSpec as P

root_coef = math.sqrt(2.0 / math.pi)
cubic_coef = 0.044715
bf16 = jnp.bfloat16
f32 = jnp.float32


def gelu_pair(pre_act, upstream):
    tanh_part = jnp.tanh(root_coef * (pre_act + cubic_coef * pre_act * pre_act * pre_act))
    activation = 0.5 * pre_act * (1.0 + tanh_part)
    slope_value = 0.5 * (1.0 + tanh_part) + 0.5 * pre_act * (
        1.0 - tanh_part * tanh_part
    ) * root_coef * (1.0 + 3.0 * cubic_coef * pre_act * pre_act)
    return (activation.astype(bf16), (upstream * slope_value).astype(bf16))


def contract_last(left, right):
    return lax.dot_general(left, right, (((1,), (1,)), ((), ())), preferred_element_type=f32)


def contract_first(left, right):
    return lax.dot_general(left, right, (((0,), (0,)), ((), ())), preferred_element_type=f32)


def vmem(mib):
    return pltpu.CompilerParams(vmem_limit_bytes=mib << 20)


def hidden_kernel(parts, bias, *refs):
    before, (grad_copies, act_out) = refs[:-2], refs[-2:]
    sums = parts[0].astype(f32)
    for j in range(1, parts.shape[0]):
        sums = sums + parts[j].astype(f32)
    act, grad = gelu_pair(sums[0] + bias[...], sums[1])
    for j in range(parts.shape[0]):
        grad_copies[j] = grad
        if before:
            act_out[j, 0] = before[0][...]
            act_out[j, 1] = act
    if not before:
        act_out[...] = act


def hidden(parts, bias, *before):
    n, pair, rows, columns = parts.shape
    tile = columns // 3
    act_shape = (n, 2, rows) if before else (rows,)
    return pl.pallas_call(
        hidden_kernel,
        grid=(columns // tile,),
        in_specs=[
            pl.BlockSpec((n, pair, rows, tile), lambda i: (0, 0, 0, i)),
            pl.BlockSpec((1, tile), lambda i: (0, i)),
        ]
        + [pl.BlockSpec((rows, tile), lambda i: (0, i))] * len(before),
        out_specs=[
            pl.BlockSpec((n, rows, tile), lambda i: (0, 0, i)),
            pl.BlockSpec((*act_shape, tile), lambda i: (*([0] * len(act_shape)), i)),
        ],
        out_shape=[
            jax.ShapeDtypeStruct((n, rows, columns), bf16),
            jax.ShapeDtypeStruct((*act_shape, columns), bf16),
        ],
        compiler_params=pltpu.CompilerParams(vmem_limit_bytes=8 << 20),
        cost_estimate=pl.CostEstimate(
            flops=40 * rows * columns,
            bytes_accessed=6 * n * rows * columns,
            transcendentals=rows * columns,
        ),
    )(parts, bias, *before)


def join_kernel(n, *refs):
    ins, outs = refs[:-n], refs[-n:]
    chunk_rows = ins[0].shape[0] // n
    chunks = [ins[j : j + n] for j in range(0, len(ins), n)]
    for c, parts in enumerate(chunks):
        total = parts[0][...]
        for part in parts[1:]:
            total = total + part[...].astype(f32)
        for k, out in enumerate(outs):
            block = total[k * chunk_rows : (k + 1) * chunk_rows]
            out[c * chunk_rows : (c + 1) * chunk_rows] = block.astype(out.dtype)


def join_sums(chunks, n):
    rows, columns = chunks[0][0].shape
    tile = columns // 3
    out_rows = len(chunks) * rows // n
    ins = [part for parts in chunks for part in parts]
    return pl.pallas_call(
        functools.partial(join_kernel, n),
        grid=(columns // tile,),
        in_specs=[pl.BlockSpec((rows, tile), lambda i: (0, i))] * len(ins),
        out_specs=[pl.BlockSpec((out_rows, tile), lambda i: (0, i))] * n,
        out_shape=[
            jax.ShapeDtypeStruct((out_rows, columns), bf16 if k else f32) for k in range(n)
        ],
        compiler_params=pltpu.CompilerParams(vmem_limit_bytes=8 << 20),
        cost_estimate=pl.CostEstimate(
            flops=len(ins) * rows * columns,
            bytes_accessed=2 * len(ins) * rows * columns,
            transcendentals=0,
        ),
    )(*ins)


def solution(mesh):
    n_x, n_y, n_z = (mesh.shape[a] for a in ("gx", "gy", "gz"))

    def shift_y(a, k):
        return lax.ppermute(a, "gy", [(i, (i + k) % n_y) for i in range(n_y)])

    def shift_chip(a, k):
        return lax.ppermute(a, "gz", [(i, (i + 2 * k) % n_z) for i in range(n_z)])

    def swap_core(a):
        return lax.ppermute(a, "gz", [(i, i ^ 1) for i in range(n_z)])

    n_chip = n_z // 2

    def groups(a):
        return [a] + [shift_y(a, k) for k in range(1, n_y)]

    def sum_blocks(parts, n):
        rows = parts[0].shape[0] // n
        sums = []
        for k in range(n):
            cut = [part[k * rows : (k + 1) * rows].astype(f32) for part in parts]
            sums.append(sum(cut[1:], cut[0]))
        return sums[:1] + [a.astype(bf16) for a in sums[1:]]

    def exchange(parts, shift):
        return [shift(part, -k) if k else part for k, part in enumerate(parts)]

    def trade_width(parts):
        return lax.all_to_all(parts, "gx", 0, 0, tiled=True)

    def after(a, *others):
        return lax.optimization_barrier((a, *others))[0]

    def join(parts):
        return jnp.concatenate(parts, axis=1)

    def barrier(*values):
        return lax.optimization_barrier(values)

    def shards(tokens, weight_in, bias_hidden, weight_out, grad_output):
        norm_scale = 1.0 / math.sqrt(tokens.shape[0] * n_y * n_z)
        rows = tokens.shape[0] // 2
        chunks = [
            jnp.stack([a[c * rows : (c + 1) * rows] for a in (tokens, grad_output)]) for c in range(2)
        ]
        bias = bias_hidden.reshape(1, -1)

        def partial_sums(pieces):
            both = [jnp.concatenate([a, swap_core(a)], axis=0) for a in join(pieces)]
            pre_part = jnp.dot(both[0], weight_in, preferred_element_type=f32).astype(bf16)
            up_part = contract_last(both[1], weight_out).astype(bf16)
            parts = [a.reshape(n_x, 1, -1, a.shape[1]) for a in (pre_part, up_part)]
            return both, jnp.concatenate(parts, axis=1)

        def two_halves(grad_hidden):
            half = grad_hidden.shape[0] // 2
            other = contract_last(grad_hidden[half:], weight_in).astype(bf16)
            return other, contract_last(grad_hidden[:half], weight_in)

        far0 = join(groups(chunks[0]))
        far1 = join(groups(after(chunks[1], far0)))
        chips0, far1 = barrier([far0] + [shift_chip(far0, k) for k in range(1, n_chip)], far1)
        both0, part0 = partial_sums(chips0)
        both1, part1 = partial_sums([far1] + [shift_chip(far1, k) for k in range(1, n_chip)])
        sums0 = trade_width(part0)
        sums1 = trade_width(part1)
        grad_copies0, act0 = hidden(sums0, bias)
        columns = act0.shape[1]
        grad_copies0, sums1 = barrier(grad_copies0, sums1)
        hidden0 = trade_width(grad_copies0)
        grad_copies1, act_copies = hidden(sums1, bias, act0)
        blocks = [a.reshape(n_x, -1, a.shape[1]) for a in (both0[1], both1[1])]
        grad_all = jnp.stack(blocks, axis=1).reshape(-1, grad_output.shape[1])
        grad_copies1, act_copies, grad_all = barrier(grad_copies1, act_copies, grad_all)
        hidden1 = trade_width(after(grad_copies1, hidden0)).reshape(-1, columns)
        hidden0 = hidden0.reshape(-1, columns)
        other0, own0 = two_halves(hidden0)
        own0, other0 = barrier(own0, swap_core(other0))
        parts0, act_copies = barrier(sum_blocks([own0, other0], n_chip), act_copies)
        parts0 = exchange(parts0, shift_chip)
        other1, own1 = two_halves(hidden1)
        parts0, other1, act_copies = barrier(parts0, other1, act_copies)
        activation = trade_width(act_copies)
        own1, other1 = barrier(own1, swap_core(other1))
        parts1, hidden0, hidden1 = barrier(sum_blocks([own1, other1], n_chip), hidden0, hidden1)
        parts1 = exchange(parts1, shift_chip)
        hidden_all = jnp.concatenate([hidden0, hidden1], axis=0)
        tokens_all = jnp.concatenate([both0[0], both1[0]], axis=0)
        grad_weight_in = (contract_first(tokens_all, hidden_all) * norm_scale).astype(bf16)
        parts0, parts1, grad_weight_in = barrier(parts0, parts1, grad_weight_in)
        parts = join_sums([parts0, parts1], n_y)
        parts = exchange(parts, shift_y)
        activation = activation.reshape(-1, columns)
        grad_weight_out = (contract_first(activation, grad_all) * norm_scale).astype(bf16)
        parts, grad_weight_out = barrier(parts, grad_weight_out)
        (grad_tokens,) = sum_blocks(parts, 1)
        return (grad_tokens.astype(bf16), grad_weight_in, grad_weight_out)

    return jax.shard_map(
        shards,
        mesh=mesh,
        in_specs=(
            P(("gy", "gz"), "gx"),
            P("gx", ("gy", "gz")),
            P(("gy", "gz")),
            P(("gy", "gz"), "gx"),
            P(("gy", "gz"), "gx"),
        ),
        out_specs=(P(("gy", "gz"), "gx"), P("gx", ("gy", "gz")), P(("gy", "gz"), "gx")),
        check_vma=False,
    )
```

```python
import functools
import math

import jax
import jax.numpy as jnp
from jax import lax
from jax.experimental import pallas as pl
from jax.experimental.pallas import tpu as pltpu
from jax.sharding import PartitionSpec as P

root_coef = math.sqrt(2.0 / math.pi)
cubic_coef = 0.044715
pre_scale = 64.0
up_scale = 128.0
bf16 = jnp.bfloat16
f16 = jnp.float16
f32 = jnp.float32


def gelu_pair(pre_act, upstream):
    tanh_part = jnp.tanh(root_coef * (pre_act + cubic_coef * pre_act * pre_act * pre_act))
    activation = 0.5 * pre_act * (1.0 + tanh_part)
    slope_value = 0.5 * (1.0 + tanh_part) + 0.5 * pre_act * (
        1.0 - tanh_part * tanh_part
    ) * root_coef * (1.0 + 3.0 * cubic_coef * pre_act * pre_act)
    return (activation.astype(bf16), (upstream * slope_value).astype(bf16))


def contract_last(left, right):
    return lax.dot_general(left, right, (((1,), (1,)), ((), ())), preferred_element_type=f32)


def contract_first(left, right):
    return lax.dot_general(left, right, (((0,), (0,)), ((), ())), preferred_element_type=f32)


def vmem(mib):
    return pltpu.CompilerParams(vmem_limit_bytes=mib << 20)


def hidden_kernel(sums, bias, *refs):
    before, (grad_copies, act_out) = refs[:-2], refs[-2:]
    act, grad = gelu_pair(sums[0] * (1.0 / pre_scale) + bias[...], sums[1] * (1.0 / up_scale))
    for j in range(grad_copies.shape[0]):
        grad_copies[j] = grad
        if before:
            act_out[j, 0] = before[0][...]
            act_out[j, 1] = act
    if not before:
        act_out[...] = act


def hidden(parts, bias, *before):
    n, pair, rows, columns = parts.shape
    sums = jnp.sum(parts.astype(f32), axis=0)
    tile = columns // 3
    act_shape = (n, 2, rows) if before else (rows,)
    return pl.pallas_call(
        hidden_kernel,
        grid=(columns // tile,),
        in_specs=[
            pl.BlockSpec((pair, rows, tile), lambda i: (0, 0, i)),
            pl.BlockSpec((1, tile), lambda i: (0, i)),
        ]
        + [pl.BlockSpec((rows, tile), lambda i: (0, i))] * len(before),
        out_specs=[
            pl.BlockSpec((n, rows, tile), lambda i: (0, 0, i)),
            pl.BlockSpec((*act_shape, tile), lambda i: (*([0] * len(act_shape)), i)),
        ],
        out_shape=[
            jax.ShapeDtypeStruct((n, rows, columns), bf16),
            jax.ShapeDtypeStruct((*act_shape, columns), bf16),
        ],
        compiler_params=pltpu.CompilerParams(vmem_limit_bytes=8 << 20),
        cost_estimate=pl.CostEstimate(
            flops=40 * rows * columns,
            bytes_accessed=6 * n * rows * columns,
            transcendentals=rows * columns,
        ),
    )(sums, bias, *before)


def join_kernel(n, n_parts, *refs):
    ins, outs = refs[:-n], refs[-n:]
    chunk_rows = ins[0].shape[0] // n
    chunks = [ins[j : j + n_parts] for j in range(0, len(ins), n_parts)]
    for c, parts in enumerate(chunks):
        total = parts[0][...]
        for part in parts[1:]:
            total = total + part[...].astype(f32)
        for k, out in enumerate(outs):
            block = total[k * chunk_rows : (k + 1) * chunk_rows]
            out[c * chunk_rows : (c + 1) * chunk_rows] = block.astype(out.dtype)


def join_sums(chunks, n, own_type=f32):
    rows, columns = chunks[0][0].shape
    tile = columns // 3
    out_rows = len(chunks) * rows // n
    ins = [part for parts in chunks for part in parts]
    return pl.pallas_call(
        functools.partial(join_kernel, n, len(chunks[0])),
        grid=(columns // tile,),
        in_specs=[pl.BlockSpec((rows, tile), lambda i: (0, i))] * len(ins),
        out_specs=[pl.BlockSpec((out_rows, tile), lambda i: (0, i))] * n,
        out_shape=[
            jax.ShapeDtypeStruct((out_rows, columns), bf16 if k else own_type) for k in range(n)
        ],
        compiler_params=pltpu.CompilerParams(vmem_limit_bytes=8 << 20),
        cost_estimate=pl.CostEstimate(
            flops=len(ins) * rows * columns,
            bytes_accessed=2 * len(ins) * rows * columns,
            transcendentals=0,
        ),
    )(*ins)


def solution(mesh):
    n_x, n_y, n_z = (mesh.shape[a] for a in ("gx", "gy", "gz"))

    def shift_y(a, k):
        return lax.ppermute(a, "gy", [(i, (i + k) % n_y) for i in range(n_y)])

    def shift_chip(a, k):
        return lax.ppermute(a, "gz", [(i, (i + 2 * k) % n_z) for i in range(n_z)])

    def swap_core(a):
        return lax.ppermute(a, "gz", [(i, i ^ 1) for i in range(n_z)])

    n_chip = n_z // 2

    def groups(a):
        return [a] + [shift_y(a, k) for k in range(1, n_y)]

    def sum_blocks(parts, n):
        rows = parts[0].shape[0] // n
        sums = []
        for k in range(n):
            cut = [part[k * rows : (k + 1) * rows].astype(f32) for part in parts]
            sums.append(sum(cut[1:], cut[0]))
        return sums[:1] + [a.astype(bf16) for a in sums[1:]]

    def exchange(parts, shift):
        return [shift(part, -k) if k else part for k, part in enumerate(parts)]

    def trade_width(parts):
        return lax.all_to_all(parts, "gx", 0, 0, tiled=True)

    def after(a, *others):
        return lax.optimization_barrier((a, *others))[0]

    def join(parts):
        return jnp.concatenate(parts, axis=1)

    def barrier(*values):
        return lax.optimization_barrier(values)

    def shards(tokens, weight_in, bias_hidden, weight_out, grad_output):
        norm_scale = 1.0 / math.sqrt(tokens.shape[0] * n_y * n_z)
        rows = tokens.shape[0] // 2
        chunks = [
            jnp.stack([a[c * rows : (c + 1) * rows] for a in (tokens, grad_output)]) for c in range(2)
        ]
        bias = bias_hidden.reshape(1, -1)

        def partial_sums(pieces):
            both = [jnp.concatenate([a, swap_core(a)], axis=0) for a in join(pieces)]
            pre_part = (jnp.dot(both[0], weight_in, preferred_element_type=f32) * pre_scale).astype(f16)
            up_part = (contract_last(both[1], weight_out) * up_scale).astype(f16)
            parts = [a.reshape(n_x, 1, -1, a.shape[1]) for a in (pre_part, up_part)]
            return both, jnp.concatenate(parts, axis=1)

        def two_halves(grad_hidden):
            half = grad_hidden.shape[0] // 2
            other = contract_last(grad_hidden[half:], weight_in).astype(bf16)
            return other, contract_last(grad_hidden[:half], weight_in)

        far0 = join(groups(chunks[0]))
        far1 = join(groups(after(chunks[1], far0)))
        chips0, far1 = barrier([far0] + [shift_chip(far0, k) for k in range(1, n_chip)], far1)
        both0, part0 = partial_sums(chips0)
        both1, part1 = partial_sums([far1] + [shift_chip(far1, k) for k in range(1, n_chip)])
        sums0 = trade_width(part0)
        sums1 = trade_width(part1)
        grad_copies0, act0 = hidden(sums0, bias)
        columns = act0.shape[1]
        grad_copies0, sums1 = barrier(grad_copies0, sums1)
        hidden0 = trade_width(grad_copies0)
        grad_copies1, act_copies = hidden(sums1, bias, act0)
        blocks = [a.reshape(n_x, -1, a.shape[1]) for a in (both0[1], both1[1])]
        grad_all = jnp.stack(blocks, axis=1).reshape(-1, grad_output.shape[1])
        grad_copies1, act_copies, grad_all = barrier(grad_copies1, act_copies, grad_all)
        hidden1 = trade_width(after(grad_copies1, hidden0)).reshape(-1, columns)
        hidden0 = hidden0.reshape(-1, columns)
        other0, own0 = two_halves(hidden0)
        own0, other0 = barrier(own0, swap_core(other0))
        parts0, act_copies = barrier(sum_blocks([own0, other0], n_chip), act_copies)
        parts0 = exchange(parts0, shift_chip)
        other1, own1 = two_halves(hidden1)
        parts0, other1, act_copies = barrier(parts0, other1, act_copies)
        activation = trade_width(act_copies)
        own1, other1 = barrier(own1, swap_core(other1))
        parts1, hidden0, hidden1 = barrier(sum_blocks([own1, other1], n_chip), hidden0, hidden1)
        parts1 = exchange(parts1, shift_chip)
        hidden_all = jnp.concatenate([hidden0, hidden1], axis=0)
        tokens_all = jnp.concatenate([both0[0], both1[0]], axis=0)
        grad_weight_in = (contract_first(tokens_all, hidden_all) * norm_scale).astype(bf16)
        parts0, grad_weight_in = barrier(parts0, grad_weight_in)
        parts0 = exchange(join_sums([parts0], n_y), shift_y)
        parts1 = exchange(join_sums([parts1], n_y), shift_y)
        activation = activation.reshape(-1, columns)
        grad_weight_out = (contract_first(activation, grad_all) * norm_scale).astype(bf16)
        parts0, parts1, grad_weight_out = barrier(parts0, parts1, grad_weight_out)
        (grad_tokens,) = join_sums([parts0, parts1], 1, bf16)
        return (grad_tokens, grad_weight_in, grad_weight_out)

    return jax.shard_map(
        shards,
        mesh=mesh,
        in_specs=(
            P(("gy", "gz"), "gx"),
            P("gx", ("gy", "gz")),
            P(("gy", "gz")),
            P(("gy", "gz"), "gx"),
            P(("gy", "gz"), "gx"),
        ),
        out_specs=(P(("gy", "gz"), "gx"), P("gx", ("gy", "gz")), P(("gy", "gz"), "gx")),
        check_vma=False,
    )
```

```python
import functools
import math

import jax
import jax.numpy as jnp
from jax import lax
from jax.experimental import pallas as pl
from jax.experimental.pallas import tpu as pltpu
from jax.sharding import PartitionSpec as P

root_coef = math.sqrt(2.0 / math.pi)
cubic_coef = 0.044715
pre_scale = 64.0
up_scale = 128.0
bf16 = jnp.bfloat16
f16 = jnp.float16
f32 = jnp.float32


def gelu_pair(pre_act, upstream):
    tanh_part = jnp.tanh(root_coef * (pre_act + cubic_coef * pre_act * pre_act * pre_act))
    activation = 0.5 * pre_act * (1.0 + tanh_part)
    slope_value = 0.5 * (1.0 + tanh_part) + 0.5 * pre_act * (
        1.0 - tanh_part * tanh_part
    ) * root_coef * (1.0 + 3.0 * cubic_coef * pre_act * pre_act)
    return (activation.astype(bf16), (upstream * slope_value).astype(bf16))


def contract_last(left, right):
    return lax.dot_general(left, right, (((1,), (1,)), ((), ())), preferred_element_type=f32)


def contract_first(left, right):
    return lax.dot_general(left, right, (((0,), (0,)), ((), ())), preferred_element_type=f32)


def vmem(mib):
    return pltpu.CompilerParams(vmem_limit_bytes=mib << 20)


def hidden_kernel(sums, bias, *refs):
    before, (grad_copies, act_out) = refs[:-2], refs[-2:]
    act, grad = gelu_pair(sums[0] * (1.0 / pre_scale) + bias[...], sums[1] * (1.0 / up_scale))
    for j in range(grad_copies.shape[0]):
        grad_copies[j] = grad
        if before:
            act_out[j, 0] = before[0][...]
            act_out[j, 1] = act
    if not before:
        act_out[...] = act


def hidden(parts, bias, *before):
    n, pair, rows, columns = parts.shape
    sums = jnp.sum(parts.astype(f32), axis=0)
    tile = columns // 3
    act_shape = (n, 2, rows) if before else (rows,)
    return pl.pallas_call(
        hidden_kernel,
        grid=(columns // tile,),
        in_specs=[
            pl.BlockSpec((pair, rows, tile), lambda i: (0, 0, i)),
            pl.BlockSpec((1, tile), lambda i: (0, i)),
        ]
        + [pl.BlockSpec((rows, tile), lambda i: (0, i))] * len(before),
        out_specs=[
            pl.BlockSpec((n, rows, tile), lambda i: (0, 0, i)),
            pl.BlockSpec((*act_shape, tile), lambda i: (*([0] * len(act_shape)), i)),
        ],
        out_shape=[
            jax.ShapeDtypeStruct((n, rows, columns), bf16),
            jax.ShapeDtypeStruct((*act_shape, columns), bf16),
        ],
        compiler_params=pltpu.CompilerParams(vmem_limit_bytes=8 << 20),
        cost_estimate=pl.CostEstimate(
            flops=40 * rows * columns,
            bytes_accessed=6 * n * rows * columns,
            transcendentals=rows * columns,
        ),
    )(sums, bias, *before)


def join_kernel(n, n_parts, *refs):
    ins, outs = refs[:-n], refs[-n:]
    chunk_rows = ins[0].shape[0] // n
    chunks = [ins[j : j + n_parts] for j in range(0, len(ins), n_parts)]
    for c, parts in enumerate(chunks):
        total = parts[0][...]
        for part in parts[1:]:
            total = total + part[...].astype(f32)
        for k, out in enumerate(outs):
            block = total[k * chunk_rows : (k + 1) * chunk_rows]
            out[c * chunk_rows : (c + 1) * chunk_rows] = block.astype(out.dtype)


def join_sums(chunks, n, own_type=f32):
    rows, columns = chunks[0][0].shape
    tile = columns // 3
    out_rows = len(chunks) * rows // n
    ins = [part for parts in chunks for part in parts]
    return pl.pallas_call(
        functools.partial(join_kernel, n, len(chunks[0])),
        grid=(columns // tile,),
        in_specs=[pl.BlockSpec((rows, tile), lambda i: (0, i))] * len(ins),
        out_specs=[pl.BlockSpec((out_rows, tile), lambda i: (0, i))] * n,
        out_shape=[
            jax.ShapeDtypeStruct((out_rows, columns), bf16 if k else own_type) for k in range(n)
        ],
        compiler_params=pltpu.CompilerParams(vmem_limit_bytes=8 << 20),
        cost_estimate=pl.CostEstimate(
            flops=len(ins) * rows * columns,
            bytes_accessed=2 * len(ins) * rows * columns,
            transcendentals=0,
        ),
    )(*ins)


def solution(mesh):
    n_x, n_y, n_z = (mesh.shape[a] for a in ("gx", "gy", "gz"))

    def shift_y(a, k):
        return lax.ppermute(a, "gy", [(i, (i + k) % n_y) for i in range(n_y)])

    def shift_chip(a, k):
        return lax.ppermute(a, "gz", [(i, (i + 2 * k) % n_z) for i in range(n_z)])

    def swap_core(a):
        return lax.ppermute(a, "gz", [(i, i ^ 1) for i in range(n_z)])

    n_chip = n_z // 2

    def groups(a):
        return [a] + [shift_y(a, k) for k in range(1, n_y)]

    def sum_blocks(parts, n):
        rows = parts[0].shape[0] // n
        sums = []
        for k in range(n):
            cut = [part[k * rows : (k + 1) * rows].astype(f32) for part in parts]
            sums.append(sum(cut[1:], cut[0]))
        return sums[:1] + [a.astype(bf16) for a in sums[1:]]

    def exchange(parts, shift):
        return [shift(part, -k) if k else part for k, part in enumerate(parts)]

    def trade_width(parts):
        return lax.all_to_all(parts, "gx", 0, 0, tiled=True)

    def after(a, *others):
        return lax.optimization_barrier((a, *others))[0]

    def join(parts):
        return jnp.concatenate(parts, axis=1)

    def barrier(*values):
        return lax.optimization_barrier(values)

    def shards(tokens, weight_in, bias_hidden, weight_out, grad_output):
        norm_scale = 1.0 / math.sqrt(tokens.shape[0] * n_y * n_z)
        rows = tokens.shape[0] // 2
        chunks = [
            jnp.stack([a[c * rows : (c + 1) * rows] for a in (tokens, grad_output)]) for c in range(2)
        ]
        bias = bias_hidden.reshape(1, -1)

        def partial_sums(pieces):
            both = [jnp.concatenate([a, swap_core(a)], axis=0) for a in join(pieces)]
            pre_part = (jnp.dot(both[0], weight_in, preferred_element_type=f32) * pre_scale).astype(f16)
            up_part = (contract_last(both[1], weight_out) * up_scale).astype(f16)
            parts = [a.reshape(n_x, 1, -1, a.shape[1]) for a in (pre_part, up_part)]
            return both, jnp.concatenate(parts, axis=1)

        def two_halves(grad_hidden):
            half = grad_hidden.shape[0] // 2
            other = contract_last(grad_hidden[half:], weight_in).astype(bf16)
            return other, contract_last(grad_hidden[:half], weight_in)

        far0 = join(groups(chunks[0]))
        far1 = join(groups(after(chunks[1], far0)))
        chips0, far1 = barrier([far0] + [shift_chip(far0, k) for k in range(1, n_chip)], far1)
        both0, part0 = partial_sums(chips0)
        both1, part1 = partial_sums([far1] + [shift_chip(far1, k) for k in range(1, n_chip)])
        sums0 = trade_width(part0)
        sums1 = trade_width(part1)
        grad_copies0, act0 = hidden(sums0, bias)
        columns = act0.shape[1]
        grad_copies0, sums1 = barrier(grad_copies0, sums1)
        hidden0 = trade_width(grad_copies0)
        grad_copies1, act_copies = hidden(sums1, bias, act0)
        blocks = [a.reshape(n_x, -1, a.shape[1]) for a in (both0[1], both1[1])]
        grad_all = jnp.stack(blocks, axis=1).reshape(-1, grad_output.shape[1])
        grad_copies1, act_copies, grad_all = barrier(grad_copies1, act_copies, grad_all)
        hidden1 = trade_width(after(grad_copies1, hidden0)).reshape(-1, columns)
        hidden0 = hidden0.reshape(-1, columns)
        other0, own0 = two_halves(hidden0)
        own0, other0 = barrier(own0, swap_core(other0))
        parts0, act_copies = barrier(sum_blocks([own0, other0], n_chip), act_copies)
        parts0 = exchange(parts0, shift_chip)
        other1, _ = two_halves(hidden1)
        parts0, other1, act_copies, hidden1 = barrier(parts0, other1, act_copies, hidden1)
        _, own1 = two_halves(hidden1)
        activation = trade_width(act_copies)
        own1, other1 = barrier(own1, swap_core(other1))
        parts1, hidden0, hidden1 = barrier(sum_blocks([own1, other1], n_chip), hidden0, hidden1)
        parts1 = exchange(parts1, shift_chip)
        hidden_all = jnp.concatenate([hidden0, hidden1], axis=0)
        tokens_all = jnp.concatenate([both0[0], both1[0]], axis=0)
        grad_weight_in = (contract_first(tokens_all, hidden_all) * norm_scale).astype(bf16)
        parts0, parts1[1] = barrier(parts0, parts1[1])
        parts0 = exchange(join_sums([parts0], n_y), shift_y)
        parts1 = exchange(join_sums([parts1], n_y), shift_y)
        activation = activation.reshape(-1, columns)
        grad_weight_out = (contract_first(activation, grad_all) * norm_scale).astype(bf16)
        parts0, parts1, *grads = barrier(parts0, parts1, grad_weight_in, grad_weight_out)
        (grad_tokens,) = join_sums([parts0, parts1], 1, bf16)
        return (grad_tokens, *grads)

    return jax.shard_map(
        shards,
        mesh=mesh,
        in_specs=(
            P(("gy", "gz"), "gx"),
            P("gx", ("gy", "gz")),
            P(("gy", "gz")),
            P(("gy", "gz"), "gx"),
            P(("gy", "gz"), "gx"),
        ),
        out_specs=(P(("gy", "gz"), "gx"), P("gx", ("gy", "gz")), P(("gy", "gz"), "gx")),
        check_vma=False,
    )
```

```python
import functools
import math

import jax
import jax.numpy as jnp
from jax import lax
from jax.experimental import pallas as pl
from jax.experimental.pallas import tpu as pltpu
from jax.sharding import PartitionSpec as P

root_coef = math.sqrt(2.0 / math.pi)
cubic_coef = 0.044715
pre_scale = 64.0
up_scale = 128.0
bf16 = jnp.bfloat16
f16 = jnp.float16
f32 = jnp.float32


def gelu_pair(pre_act, upstream):
    tanh_part = jnp.tanh(root_coef * (pre_act + cubic_coef * pre_act * pre_act * pre_act))
    activation = 0.5 * pre_act * (1.0 + tanh_part)
    slope_value = 0.5 * (1.0 + tanh_part) + 0.5 * pre_act * (
        1.0 - tanh_part * tanh_part
    ) * root_coef * (1.0 + 3.0 * cubic_coef * pre_act * pre_act)
    return (activation.astype(bf16), (upstream * slope_value).astype(bf16))


def contract_last(left, right):
    return lax.dot_general(left, right, (((1,), (1,)), ((), ())), preferred_element_type=f32)


def contract_first(left, right):
    return lax.dot_general(left, right, (((0,), (0,)), ((), ())), preferred_element_type=f32)


def vmem(mib):
    return pltpu.CompilerParams(vmem_limit_bytes=mib << 20)


def hidden_kernel(sums, bias, *refs):
    before, (grad_copies, act_out) = refs[:-2], refs[-2:]
    act, grad = gelu_pair(sums[0] * (1.0 / pre_scale) + bias[...], sums[1] * (1.0 / up_scale))
    for j in range(grad_copies.shape[0]):
        grad_copies[j] = grad
        if before:
            act_out[j, 0] = before[0][...]
            act_out[j, 1] = act
    if not before:
        act_out[...] = act


def hidden(parts, bias, *before):
    n, pair, rows, columns = parts.shape
    sums = jnp.sum(parts.astype(f32), axis=0)
    tile = columns // 3
    act_shape = (n, 2, rows) if before else (rows,)
    return pl.pallas_call(
        hidden_kernel,
        grid=(columns // tile,),
        in_specs=[
            pl.BlockSpec((pair, rows, tile), lambda i: (0, 0, i)),
            pl.BlockSpec((1, tile), lambda i: (0, i)),
        ]
        + [pl.BlockSpec((rows, tile), lambda i: (0, i))] * len(before),
        out_specs=[
            pl.BlockSpec((n, rows, tile), lambda i: (0, 0, i)),
            pl.BlockSpec((*act_shape, tile), lambda i: (*([0] * len(act_shape)), i)),
        ],
        out_shape=[
            jax.ShapeDtypeStruct((n, rows, columns), bf16),
            jax.ShapeDtypeStruct((*act_shape, columns), bf16),
        ],
        compiler_params=pltpu.CompilerParams(vmem_limit_bytes=8 << 20),
        cost_estimate=pl.CostEstimate(
            flops=40 * rows * columns,
            bytes_accessed=6 * n * rows * columns,
            transcendentals=rows * columns,
        ),
    )(sums, bias, *before)


def join_kernel(n, n_parts, *refs):
    ins, outs = refs[:-n], refs[-n:]
    chunk_rows = ins[0].shape[0] // n
    chunks = [ins[j : j + n_parts] for j in range(0, len(ins), n_parts)]
    for c, parts in enumerate(chunks):
        total = parts[0][...]
        for part in parts[1:]:
            total = total + part[...].astype(f32)
        for k, out in enumerate(outs):
            block = total[k * chunk_rows : (k + 1) * chunk_rows]
            out[c * chunk_rows : (c + 1) * chunk_rows] = block.astype(out.dtype)


def join_sums(chunks, n, own_type=f32):
    rows, columns = chunks[0][0].shape
    tile = columns // 3
    out_rows = len(chunks) * rows // n
    ins = [part for parts in chunks for part in parts]
    return pl.pallas_call(
        functools.partial(join_kernel, n, len(chunks[0])),
        grid=(columns // tile,),
        in_specs=[pl.BlockSpec((rows, tile), lambda i: (0, i))] * len(ins),
        out_specs=[pl.BlockSpec((out_rows, tile), lambda i: (0, i))] * n,
        out_shape=[
            jax.ShapeDtypeStruct((out_rows, columns), bf16 if k else own_type) for k in range(n)
        ],
        compiler_params=pltpu.CompilerParams(vmem_limit_bytes=8 << 20),
        cost_estimate=pl.CostEstimate(
            flops=len(ins) * rows * columns,
            bytes_accessed=2 * len(ins) * rows * columns,
            transcendentals=0,
        ),
    )(*ins)


def solution(mesh):
    n_x, n_y, n_z = (mesh.shape[a] for a in ("gx", "gy", "gz"))

    def shift_y(a, k):
        return lax.ppermute(a, "gy", [(i, (i + k) % n_y) for i in range(n_y)])

    def shift_chip(a, k):
        return lax.ppermute(a, "gz", [(i, (i + 2 * k) % n_z) for i in range(n_z)])

    def swap_core(a):
        return lax.ppermute(a, "gz", [(i, i ^ 1) for i in range(n_z)])

    n_chip = n_z // 2

    def groups(a):
        return [a] + [shift_y(a, k) for k in range(1, n_y)]

    def sum_blocks(parts, n):
        rows = parts[0].shape[0] // n
        sums = []
        for k in range(n):
            cut = [part[k * rows : (k + 1) * rows].astype(f32) for part in parts]
            sums.append(sum(cut[1:], cut[0]))
        return sums[:1] + [a.astype(bf16) for a in sums[1:]]

    def exchange(parts, shift):
        return [shift(part, -k) if k else part for k, part in enumerate(parts)]

    def trade_width(parts):
        return lax.all_to_all(parts, "gx", 0, 0, tiled=True)

    def after(a, *others):
        return lax.optimization_barrier((a, *others))[0]

    def join(parts):
        return jnp.concatenate(parts, axis=1)

    def barrier(*values):
        return lax.optimization_barrier(values)

    def shards(tokens, weight_in, bias_hidden, weight_out, grad_output):
        norm_scale = 1.0 / math.sqrt(tokens.shape[0] * n_y * n_z)
        rows = tokens.shape[0] // 2
        chunks = [
            jnp.stack([a[c * rows : (c + 1) * rows] for a in (tokens, grad_output)]) for c in range(2)
        ]
        bias = bias_hidden.reshape(1, -1)

        def partial_sums(pieces):
            both = [jnp.concatenate([a, swap_core(a)], axis=0) for a in join(pieces)]
            pre_part = (jnp.dot(both[0], weight_in, preferred_element_type=f32) * pre_scale).astype(f16)
            up_part = (contract_last(both[1], weight_out) * up_scale).astype(f16)
            parts = [a.reshape(n_x, 1, -1, a.shape[1]) for a in (pre_part, up_part)]
            return both, jnp.concatenate(parts, axis=1)

        def two_halves(grad_hidden):
            half = grad_hidden.shape[0] // 2
            other = contract_last(grad_hidden[half:], weight_in).astype(bf16)
            return other, contract_last(grad_hidden[:half], weight_in)

        far0 = join(groups(chunks[0]))
        far1 = join(groups(after(chunks[1], far0)))
        chips0, far1 = barrier([far0] + [shift_chip(far0, k) for k in range(1, n_chip)], far1)
        both0, part0 = partial_sums(chips0)
        both1, part1 = partial_sums([far1] + [shift_chip(far1, k) for k in range(1, n_chip)])
        sums0 = trade_width(part0)
        sums1 = trade_width(part1)
        grad_copies0, act0 = hidden(sums0, bias)
        columns = act0.shape[1]
        grad_copies0, sums1 = barrier(grad_copies0, sums1)
        hidden0 = trade_width(grad_copies0)
        grad_copies1, act_copies = hidden(sums1, bias, act0)
        blocks = [a.reshape(n_x, -1, a.shape[1]) for a in (both0[1], both1[1])]
        grad_all = jnp.stack(blocks, axis=1).reshape(-1, grad_output.shape[1])
        grad_copies1, act_copies, grad_all = barrier(grad_copies1, act_copies, grad_all)
        hidden1 = trade_width(after(grad_copies1, hidden0)).reshape(-1, columns)
        hidden0 = hidden0.reshape(-1, columns)
        other0, own0 = two_halves(hidden0)
        own0, other0 = barrier(own0, swap_core(other0))
        parts0, act_copies = barrier(sum_blocks([own0, other0], n_chip), act_copies)
        parts0 = exchange(parts0, shift_chip)
        other1, _ = two_halves(hidden1)
        parts0[:-1], other1, act_copies, hidden1 = barrier(
            parts0[:-1], other1, act_copies, hidden1
        )
        _, own1 = two_halves(hidden1)
        activation = trade_width(act_copies)
        own1, other1 = barrier(own1, swap_core(other1))
        parts1, hidden0, hidden1 = barrier(sum_blocks([own1, other1], n_chip), hidden0, hidden1)
        parts1 = exchange(parts1, shift_chip)
        hidden_all = jnp.concatenate([hidden0, hidden1], axis=0)
        tokens_all = jnp.concatenate([both0[0], both1[0]], axis=0)
        grad_weight_in = (contract_first(tokens_all, hidden_all) * norm_scale).astype(bf16)
        parts0, grad_weight_in = barrier(parts0, grad_weight_in)
        parts0 = exchange(join_sums([parts0], n_y), shift_y)
        parts1 = exchange(join_sums([parts1], n_y), shift_y)
        activation = activation.reshape(-1, columns)
        grad_weight_out = (contract_first(activation, grad_all) * norm_scale).astype(bf16)
        parts0, parts1, grad_weight_out = barrier(parts0, parts1, grad_weight_out)
        (grad_tokens,) = join_sums([parts0, parts1], 1, bf16)
        return (grad_tokens, grad_weight_in, grad_weight_out)

    return jax.shard_map(
        shards,
        mesh=mesh,
        in_specs=(
            P(("gy", "gz"), "gx"),
            P("gx", ("gy", "gz")),
            P(("gy", "gz")),
            P(("gy", "gz"), "gx"),
            P(("gy", "gz"), "gx"),
        ),
        out_specs=(P(("gy", "gz"), "gx"), P("gx", ("gy", "gz")), P(("gy", "gz"), "gx")),
        check_vma=False,
    )
```
